1024 devices in a mesh: grp: 16 (over y, core), emb: 64 (over x, z).
Axes of the slice: x: 8, y: 8, z: 8, core: 2. Of those that a mesh axis runs over, the one named last changes fastest.
Arguments:
- table_window: bfloat16 [131072, 128], P('emb'), may hold values from -3 to 3
- dense_part: bfloat16 [131072, 128], P(('grp', 'emb')), may hold values from -6 to 6
- bag_rows: int32 [131072, 26, 8], P(('grp', 'emb')), may hold values from 0 to 2047
- bag_lengths: int32 [131072, 26], P(('grp', 'emb')), may hold values from 1 to 8
- bag_owner: int32 [131072, 26, 1], P(('grp', 'emb')), may hold values from 0 to 63; in each aligned block of 3328 rows (0 to 3327, 3328 to 6655, ..., all dimensions but the last counted through in order) at most 78 rows name the same one
- labels: int32 [131072], P(('grp', 'emb')), may hold values 0 or 1
- sample_weight: float32 [131072], P(('grp', 'emb')), may hold values from 0.005 to 1.5
- down_w: bfloat16 [3456, 512], replicated, may hold values from -0.109375 to 0.109375
- up_w: bfloat16 [512, 3456], replicated, may hold values from -0.25 to 0.25
- cross_bias: float32 [3456], replicated, may hold values from -3 to 3
- head_w: float32 [3456], replicated, may hold values from -0.109375 to 0.109375
Outputs:
- row_grad: float32 [131072, 128], P('emb')
- head_grad: float32 [3456], replicated
- bias_grad: float32 [3456], replicated
- dense_grad: bfloat16 [131072, 128], P(('grp', 'emb'))
The draws below stay inside these ranges and needn't reach their ends.
Inputs may be any that keep to these rules, and one draw needn't show every extreme that they name: `bag_owner`: among the bags of the samples of one device (aligned blocks of 128 samples), at most 78 have one owner, and some owner has exactly 78.
All inputs are finite; a program needn't handle non-finite values. No bound on the sum of `labels` on one device may be relied on, other than what follows from the above.
Results may differ from the reference program's by a relative error of at most 0.0045.
The reference program's roundings to bfloat16 on the way (of `pooled`, `x0`, `low`, `d_cross`, `d_low` and `d_pooled`) count: a program that leaves them out, or rounds other values in their place, can miss the bound.
Values may be sent and summed in bfloat16 or wider, within the bound.
A program may use at most 128 MiB of HBM per device.

```python
import math
import jax
import jax.numpy as jnp
import numpy as np
from jax import lax

D_EMB = 128
TABLES = 26
RANK = 512
HOT = 8
SAMP = 128
LOCAL_ROWS = 2048
CROSS = 3456
CAP = 78
BATCH = 131072
WINDOW = 131072
N_EMB = 64


def draw_sample_weight(key, part):
    key = jax.random.fold_in(key, 11)
    position = jnp.arange(BATCH, dtype=jnp.float32) / BATCH
    falling = jnp.exp(-math.log(100.0) * position)
    jitter = jax.random.uniform(key, (BATCH,), jnp.float32, 0.7, 1.3)
    return (falling * jitter).astype(jnp.float32)


def set_ends(result, stream_key, low, high):
    spot = [jax.random.randint(jax.random.fold_in(stream_key, axis), (), 0, length) for axis, length in enumerate(result.shape)]
    main_axis = result.shape.index(max(result.shape))
    beside = spot[:main_axis] + [(spot[main_axis] + 1) % result.shape[main_axis]] + spot[main_axis + 1:]
    return result.at[tuple(spot)].set(low).at[tuple(beside)].set(high)


def levels(own_key, extent, pieces, smallest, largest):
    level, own = 1.0, jax.random.fold_in(own_key, 6)
    for dim, parts in pieces:
        steps = jnp.exp(jax.random.uniform(jax.random.fold_in(own, dim), (parts,), jnp.float32, smallest / len(pieces), largest / len(pieces)))
        level = level * jnp.repeat(steps, extent[dim] // parts).reshape([-1 if axis == dim else 1 for axis in range(len(extent))])
    return level


def routed_block(own_key, own, number, rows, count, top, reach, skew):
    ranking = jax.random.permutation(own_key, count)
    heavy_load, usual = load_shares(count, rows * top, reach, skew, True), load_shares(count, rows * top, reach, skew, False)
    places = jnp.arange(count)

    def named(tallies, rotation):
        used = int((tallies > 0).sum())
        fixed = max(1, used // 4)
        moved = fixed + (places - fixed + rotation * (used - fixed)) % max(1, count - fixed)
        return jnp.zeros((count,), jnp.int32).at[ranking[jnp.where(places < fixed, places, moved)]].set(jnp.asarray(tallies, jnp.int32))

    tallies = jnp.where(number % 4 == 0, named(heavy_load, number // 4), named(usual, number - number // 4 - 1))
    mixed = jax.random.permutation(jax.random.fold_in(own, 3), count)
    source_of, taker = mixed[0:count // 2 * 2:2], mixed[1:count // 2 * 2:2]
    margin = jnp.minimum(tallies[source_of] - 1, reach - tallies[taker]) // 2
    margin = jnp.where((source_of == ranking[0]) | (taker == ranking[0]) | (tallies[taker] == 0), 0, jnp.maximum(margin, 0))
    moved = jax.random.randint(jax.random.fold_in(own, 4), (count // 2,), 0, 1 << 20) % (margin + 1)
    tallies = tallies.at[source_of].add(-moved).at[taker].add(moved)
    items = jnp.searchsorted(jnp.cumsum(tallies), jnp.arange(rows * top), side="right").astype(jnp.int32)
    grid = items.reshape(top, rows).T
    grid = grid[jax.random.permutation(jax.random.fold_in(own, 1), rows)]
    rotation = jax.random.randint(jax.random.fold_in(own, 2), (rows, 1), 0, top)
    return jnp.take_along_axis(grid, (jnp.arange(top)[None, :] + rotation) % top, axis=1)


def load_shares(count, total, most, skew, full):
    portions = [(1 << 20) // math.isqrt(standing ** skew) + 1 for standing in range(1, count + 1)]
    largest = most if full else min(most, max(-(-total // count), total * portions[0] // sum(portions)))
    least = 1 if total - largest >= count - 1 else 0
    holding, spare = [largest] + [least] * (count - 1), total - largest - least * (count - 1)
    while spare > 0:
        free = [i for i in range(1, count) if holding[i] < largest] or [i for i in range(1, count) if holding[i] < most]
        mass, budget = sum([portions[i] for i in free]), spare
        for i in free:
            more = min(most - holding[i], max(1, budget * portions[i] // mass), spare)
            holding[i] = holding[i] + more
            spare = spare - more
    return np.array(holding)


def normal_values(key, shape, deviation, reach, cuts=(), kind=jnp.bfloat16):
    values = deviation * jax.random.normal(key, shape, jnp.float32)
    if cuts:
        values = values * levels(key, shape, cuts, -0.22, 0.18)
    return jnp.clip(values, -reach, reach).astype(kind)


def setup_inputs(seed: int = 0) -> dict:
    seeds = jax.random.split(jax.random.key(seed), 12)
    table_window = normal_values(seeds[0], (WINDOW, D_EMB), 0.5, 3.0, ((0, 64),))
    dense_part = normal_values(seeds[1], (BATCH, D_EMB), 1.0, 6.0, ((0, 1024),))
    bag_rows = set_ends(jax.random.randint(seeds[2], (BATCH, TABLES, HOT), 0, LOCAL_ROWS), jax.random.fold_in(seeds[2], 1), 0, LOCAL_ROWS - 1).astype(jnp.int32)
    bag_lengths = set_ends(jax.random.randint(seeds[3], (BATCH, TABLES), 1, HOT + 1), jax.random.fold_in(seeds[3], 1), 1, HOT).astype(jnp.int32)
    bag_owner_keys = jax.random.split(jax.random.fold_in(seeds[4], 1), BATCH * TABLES // (SAMP * TABLES))
    bag_owner_turns = jax.random.permutation(jax.random.fold_in(seeds[4], 3), BATCH * TABLES // (SAMP * TABLES))
    bag_owner = jax.vmap(lambda own, number: routed_block(jax.random.fold_in(seeds[4], 2), own, number, SAMP * TABLES, N_EMB, 1, CAP, 2))(bag_owner_keys, bag_owner_turns).reshape((BATCH, TABLES, 1))
    labels = set_ends((jax.random.randint(seeds[5], (BATCH,), 0, 4) < 1).astype(jnp.int32), jax.random.fold_in(seeds[5], 1), 0, 1)
    sample_weight = draw_sample_weight(jax.random.fold_in(seeds[11], 71), 0)
    down_w = normal_values(seeds[7], (CROSS, RANK), CROSS ** -0.5, 0.109375)
    up_w = normal_values(seeds[8], (RANK, CROSS), RANK ** -0.5, 0.25)
    cross_bias = normal_values(seeds[9], (CROSS,), 0.5, 3.0, (), jnp.float32)
    head_w = normal_values(seeds[10], (CROSS,), CROSS ** -0.5, 0.109375, (), jnp.float32)
    return {"table_window": table_window, "dense_part": dense_part, "bag_rows": bag_rows, "bag_lengths": bag_lengths, "bag_owner": bag_owner, "labels": labels, "sample_weight": sample_weight, "down_w": down_w, "up_w": up_w, "cross_bias": cross_bias, "head_w": head_w}


def reference(table_window, dense_part, bag_rows, bag_lengths, bag_owner, labels, sample_weight, down_w, up_w, cross_bias, head_w):
    block = SAMP * 8
    blocks = BATCH // block
    hot_pos = jnp.arange(HOT, dtype=jnp.int32)

    def step(carry, index):
        row_acc, head_acc, bias_acc = carry
        start = (index * block).astype(jnp.int32)
        rows = lax.dynamic_slice_in_dim(bag_rows, start, block, 0)
        lens = lax.dynamic_slice_in_dim(bag_lengths, start, block, 0)
        owner = lax.dynamic_slice_in_dim(bag_owner, start, block, 0)
        dense = lax.dynamic_slice_in_dim(dense_part, start, block, 0)
        label = lax.dynamic_slice_in_dim(labels, start, block, 0)
        weight = lax.dynamic_slice_in_dim(sample_weight, start, block, 0)
        place = owner[:, :, 0][:, :, None] * LOCAL_ROWS + rows
        live = hot_pos[None, None, :] < lens[:, :, None]
        safe = jnp.where(live, place, 0).astype(jnp.int32)
        gathered = table_window[safe].astype(jnp.float32) * live[..., None].astype(jnp.float32)
        pooled = jnp.sum(gathered, axis=2).astype(jnp.bfloat16).reshape(block, TABLES * D_EMB)
        x0 = jnp.concatenate([dense, pooled], axis=1)
        low = jnp.dot(x0, down_w, preferred_element_type=jnp.float32).astype(jnp.bfloat16)
        cross = jnp.dot(low, up_w, preferred_element_type=jnp.float32) + cross_bias[None, :]
        x0f = x0.astype(jnp.float32)
        x1 = x0f * cross + x0f
        logit = jnp.dot(x1, head_w, precision=lax.Precision.HIGHEST)
        dlogit = weight * (jax.nn.sigmoid(logit) - label.astype(jnp.float32))
        d_x1 = dlogit[:, None] * head_w[None, :]
        head_acc = head_acc + jnp.dot(dlogit, x1, precision=lax.Precision.HIGHEST)
        bias_acc = bias_acc + jnp.sum(d_x1 * x0f, axis=0)
        d_cross = (d_x1 * x0f).astype(jnp.bfloat16)
        d_low = jnp.dot(d_cross, up_w.T, preferred_element_type=jnp.float32).astype(jnp.bfloat16)
        d_x0 = d_x1 * (cross + 1.0) + jnp.dot(d_low, down_w.T, preferred_element_type=jnp.float32)
        d_pooled = d_x0[:, D_EMB:].astype(jnp.bfloat16).reshape(block, TABLES, D_EMB)
        contrib = d_pooled.astype(jnp.float32)[:, :, None, :] * live[..., None].astype(jnp.float32)
        row_acc = row_acc.at[safe.reshape(-1)].add(contrib.reshape(-1, D_EMB))
        return (row_acc, head_acc, bias_acc), d_x0[:, :D_EMB].astype(jnp.bfloat16)

    init = (jnp.zeros((WINDOW, D_EMB), jnp.float32), jnp.zeros((CROSS,), jnp.float32), jnp.zeros((CROSS,), jnp.float32))
    (row_grad, head_grad, bias_grad), dense_blocks = lax.scan(step, init, jnp.arange(blocks, dtype=jnp.int32))
    return row_grad, head_grad, bias_grad, dense_blocks.reshape(BATCH, D_EMB)
```

```python
import functools

import jax
import jax.numpy as jnp
from jax import lax
from jax.experimental import pallas as pl
from jax.experimental.pallas import tpu as pltpu
from jax.sharding import PartitionSpec as P

MESH = pl.DeviceIdType.MESH
F32 = jnp.float32
BF16 = jnp.bfloat16
I32 = jnp.int32
NT = (((1,), (1,)), ((), ()))
LAG = 2


def iota(shape, dim):
    return lax.broadcasted_iota(I32, shape, dim)


def hot(mask):
    return jnp.where(mask, 1.0, 0.0).astype(BF16)


def kernel(
    ring, tables, slots, pairs,
    own_ref, len_ref, rows_ref, label_ref, weight_ref, dense_ref, table_ref, bias_ref, head_ref,
    down_any, up_any,
    rg_ref, hb_ref, dg_ref,
    down, up, pos_row, pos_col, req_acc, code_s, code_r, counts, pool_s, pool_r, grad_s, grad_r,
    x0, x0_acc, cross, d_pool, chunk_acc, acc, pair_r, rs_r,
    hb, h1, h2, h3, h4,
    w_sem, code_ss, code_rs, pool_ss, pool_rs, grad_ss, grad_rs,
    pr_ss, pr_rs, rs_ss, rs_rs, ag_ss, ag_rs, pa_ss, pa_rs, h_ss, h_rs,
):
    peers = ring * ring
    groups = 2 * pairs
    chunk = ring * slots
    bits = ring.bit_length() - 1
    code_rows = slots * 8 // 128
    local_rows, width = table_ref.shape
    block = local_rows // groups
    tiles = tables + 1
    me = lax.axis_index("emb")
    grp = lax.axis_index("grp")
    x, z = me // ring, lax.rem(me, ring)
    y, c = grp // 2, lax.rem(grp, 2)
    mate = {"grp": grp + 1 - 2 * c}

    def ahead(k):
        dx = lax.rem(k, ring)
        dz = lax.rem(dx + k // ring, ring)
        return {"emb": lax.rem(x + dx, ring) * ring + lax.rem(z + dz, ring)}

    def behind(k):
        dx = lax.rem(k, ring)
        dz = lax.rem(dx + k // ring, ring)
        return {"emb": lax.rem(x + ring - dx, ring) * ring + lax.rem(z + ring - dz, ring)}

    def along_x(d):
        return {"emb": lax.rem(x + d, ring) * ring + z}

    def along_z(d):
        return {"emb": x * ring + lax.rem(z + d, ring)}

    def along_y(d):
        return {"grp": lax.rem(y + d, pairs) * 2 + c}

    def remote(src, dst, send, recv, where):
        return pltpu.make_async_remote_copy(
            src_ref=src, dst_ref=dst, send_sem=send, recv_sem=recv, device_id=where, device_id_type=MESH
        )

    def loop(low, high, step):
        def run(i, carry):
            step(i)
            return carry

        lax.fori_loop(low, high, run, 0)

    down_copy = pltpu.make_async_copy(down_any, down, w_sem.at[0])
    up_copy = pltpu.make_async_copy(up_any, up, w_sem.at[1])
    down_copy.start()
    up_copy.start()

    barrier = pltpu.get_barrier_semaphore()
    loop(1, peers, lambda k: pl.semaphore_signal(barrier, inc=1, device_id=ahead(k), device_id_type=MESH))
    loop(1, pairs, lambda d: pl.semaphore_signal(barrier, inc=1, device_id=along_y(d), device_id_type=MESH))
    pl.semaphore_signal(barrier, inc=1, device_id=mate, device_id_type=MESH)

    req_acc[...] = jnp.zeros_like(req_acc)
    upper = jnp.concatenate([hot(iota((128, 128), 0) < iota((128, 128), 1)), jnp.ones((128, 128), BF16)], axis=1)

    def bucket(t, carry):
        owner = own_ref[pl.ds(t, 1), :]
        dx = ((owner >> bits) - x) & (ring - 1)
        dz = ((owner & (ring - 1)) - z) & (ring - 1)
        kind = ((dz - dx) & (ring - 1)) * ring + dx
        mine = iota((128, 128), 0) == kind
        mine_f = jnp.where(mine, 1.0, 0.0)
        sums = jnp.dot(mine_f.astype(BF16), upper, preferred_element_type=F32)
        slot = jnp.sum(mine_f * (sums[:, :128] + carry), axis=0, keepdims=True).astype(I32)
        pos_row[pl.ds(t, 1), :] = kind * slots + slot
        live = iota((8, 128), 0) < len_ref[pl.ds(t, 1), :]
        code = jnp.where(live, rows_ref[pl.ds(pl.multiple_of(t * 8, 8), 8), :] + 1, 0)
        high = (code >> 4).astype(F32)
        low = (code & 15).astype(F32)
        here = [slot == s for s in range(slots)]
        spread = jnp.concatenate(
            [jnp.where(h, high, 0.0) for h in here] + [jnp.where(h, low, 0.0) for h in here], axis=0
        ).astype(BF16)
        req_acc[...] += lax.dot_general(spread, mine_f.astype(BF16), NT, preferred_element_type=F32)
        return carry + sums[:, 128:]

    lax.fori_loop(0, tables, bucket, jnp.zeros((128, 128), F32))
    for p in range(code_rows):
        high = req_acc[p * 128:(p + 1) * 128, :]
        low = req_acc[slots * 8 + p * 128:slots * 8 + (p + 1) * 128, :]
        tile = (high * 16.0 + low - 1.0).T
        code_s[pl.ds(p, peers, stride=8), :] = tile[:peers].astype(I32)

    pl.semaphore_wait(barrier, peers - 1 + pairs - 1 + 1)

    def code_copy(k):
        part = pl.ds(pl.multiple_of(k * 8, 8), 8)
        return remote(code_s.at[part], code_r.at[part], code_ss.at[k], code_rs.at[k], ahead(k))

    def pool_copy(k):
        part = pl.ds(pl.multiple_of(k * slots, 16), slots)
        return remote(pool_s.at[part], pool_r.at[part], pool_ss.at[k], pool_rs.at[k], behind(k))

    def grad_copy(k):
        part = pl.ds(pl.multiple_of(k * slots, 16), slots)
        return remote(grad_s.at[part], grad_r.at[part], grad_ss.at[k], grad_rs.at[k], ahead(k))

    loop(1, peers, lambda k: code_copy(k).start())
    code_r[0:8, :] = code_s[0:8, :]

    def turn(t):
        row = jnp.broadcast_to(pos_row[pl.ds(t, 1), :], (128, 128)).astype(F32)
        pos_col[pl.ds(pl.multiple_of(t * 128, 128), 128), :] = row.T.astype(I32)
        x0_acc[pl.ds(pl.multiple_of(t * 128, 128), 128), :] = jnp.zeros((128, 128), F32)

    loop(0, tables, turn)
    acc[...] = jnp.zeros_like(acc)

    def count_bags(k):
        tile = code_r[pl.ds(pl.multiple_of(k * 8, 8), 8), :]
        base = pl.multiple_of(k * slots, 16)
        for first in range(0, code_rows, 2):
            last = min(first + 2, code_rows)
            code = jnp.concatenate([tile[p:p + 1, :] for p in range(first, last)], axis=1)
            bags = (last - first) * 16
            lanes = bags * 8
            spans = local_rows // 256
            key = (code >> 8) * bags + (iota((1, lanes), 1) >> 3)
            left = hot(iota((spans * bags, lanes), 0) == key)
            right = hot(iota((256, lanes), 0) == (code & 255))
            out = lax.dot_general(left, right, NT, preferred_element_type=F32).astype(BF16)
            for s in range(spans):
                counts[pl.ds(base + first * 16, bags), s * 256:(s + 1) * 256] = out[s * bags:(s + 1) * bags, :]

    def pool_chunk(j):
        def one(i):
            k = j * ring + i

            @pl.when(k != 0)
            def _():
                code_copy(k).wait_recv()

            count_bags(k)

        loop(0, ring, one)
        part = pl.ds(pl.multiple_of(j * chunk, 16), chunk)
        pool_s[part, :] = jnp.dot(counts[part, :], table_ref[...], preferred_element_type=F32).astype(BF16)

        def send(i):
            k = j * ring + i

            @pl.when(k != 0)
            def _():
                pool_copy(k).start()

        loop(0, ring, send)

        @pl.when(j == 0)
        def _():
            pool_r[0:slots, :] = pool_s[0:slots, :]

    def place_chunk(j):
        def one(i):
            k = j * ring + i

            @pl.when(k != 0)
            def _():
                pool_copy(k).wait_recv()

        loop(0, ring, one)
        part = pl.ds(pl.multiple_of(j * chunk, 16), chunk)

        def some(t):
            rows = pl.ds(pl.multiple_of(t * 256, 256), 256)
            column = pos_col[rows, :] - j * chunk
            pick = jnp.concatenate([hot(column == iota((256, 128), 1) + q) for q in range(0, chunk, 128)], axis=1)
            x0_acc[rows, :] += jnp.dot(pick, pool_r[part, :], preferred_element_type=F32)

        loop(0, tables // 2, some)

    def forward(j):
        pool_chunk(j)

        @pl.when(j >= LAG)
        def _():
            place_chunk(j - LAG)

    loop(0, ring, forward)
    loop(ring - LAG, ring, place_chunk)

    down_copy.wait()
    up_copy.wait()
    x0[:, :width] = dense_ref[...]
    for t in range(tables):
        x0[:, (t + 1) * width:(t + 2) * width] = x0_acc[t * 128:(t + 1) * 128, :].astype(BF16)
    step = 3 * width
    cuts = range(0, tiles * width, step)
    low = jnp.zeros((128, down.shape[1]), F32)
    for a in cuts:
        low = low + jnp.dot(x0[:, a:a + step], down[a:a + step, :], preferred_element_type=F32)
    low = low.astype(BF16)
    logit_acc = jnp.zeros((128, width), F32)
    for a in cuts:
        part = jnp.dot(low, up[:, a:a + step], preferred_element_type=F32) + bias_ref[:, a:a + step]
        cross[:, a:a + step] = part
        x0f = x0[:, a:a + step].astype(F32)
        term = (x0f * part + x0f) * head_ref[:, a:a + step]
        for b in range(0, step, width):
            logit_acc = logit_acc + term[:, b:b + width]
    logit = jnp.sum(logit_acc, axis=1, keepdims=True)
    label = jnp.broadcast_to(label_ref[...].astype(F32), (128, 128)).T[:, 0:1]
    weight = jnp.broadcast_to(weight_ref[...], (128, 128)).T[:, 0:1]
    dlogit = weight * (jax.nn.sigmoid(logit) - label)
    hb[...] = jnp.zeros_like(hb)
    d_low = jnp.zeros((128, down.shape[1]), F32)
    for a in cuts:
        x0f = x0[:, a:a + step].astype(F32)
        x1 = x0f * cross[:, a:a + step] + x0f
        d_cross = dlogit * head_ref[:, a:a + step] * x0f
        head_part = jnp.sum(dlogit * x1, axis=0, keepdims=True)
        bias_part = jnp.sum(d_cross, axis=0, keepdims=True)
        for b in range(0, step, width):
            r = (a + b) // width
            hb[r:r + 1, :] = head_part[:, b:b + width]
            hb[tiles + r:tiles + r + 1, :] = bias_part[:, b:b + width]
        d_low = d_low + lax.dot_general(d_cross.astype(BF16), up[:, a:a + step], NT, preferred_element_type=F32)
    d_low = d_low.astype(BF16)

    def h_part(r):
        return pl.ds(pl.multiple_of(r * 8, 8), 8)

    def h1_copy(d):
        return remote(hb.at[h_part(lax.rem(x + d, ring))], h1.at[h_part(d)], h_ss.at[0, d], h_rs.at[0, d], along_x(d))

    def h2_copy(d):
        return remote(h2.at[h_part(z)], h2.at[h_part(z)], h_ss.at[1, d], h_rs.at[1, d], along_z(d))

    def h3_copy(d):
        return remote(h3.at[h_part(y)], h3.at[h_part(y)], h_ss.at[2, d], h_rs.at[2, d], along_y(d))

    def h4_copy():
        return remote(h4.at[h_part(c)], h4.at[h_part(c)], h_ss.at[3, 0], h_rs.at[3, 0], mate)

    def h5_copy(d):
        return remote(hb_ref.at[h_part(x)], hb_ref.at[h_part(x)], h_ss.at[4, d], h_rs.at[4, d], along_x(d))

    loop(1, ring, lambda d: h1_copy(d).start())

    def total_of(ref, count, start=0):
        total = ref[start * 8:start * 8 + 8, :]
        for r in range(start + 1, count):
            total = total + ref[r * 8:r * 8 + 8, :]
        return total

    def h_step1():
        loop(1, ring, lambda d: h1_copy(d).wait_recv())
        h2[h_part(z), :] = total_of(h1, ring, 1) + hb[h_part(x), :]
        loop(1, ring, lambda d: h2_copy(d).start())

    def h_step2():
        loop(1, ring, lambda d: h2_copy(d).wait_recv())
        h3[h_part(y), :] = total_of(h2, ring)
        loop(1, pairs, lambda d: h3_copy(d).start())

    def h_step3():
        loop(1, pairs, lambda d: h3_copy(d).wait_recv())
        h4[h_part(c), :] = total_of(h3, pairs)
        h4_copy().start()

    def h_step4():
        h4_copy().wait_recv()
        hb_ref[h_part(x), :] = total_of(h4, 2)
        loop(1, ring, lambda d: h5_copy(d).start())

    for a in cuts:
        d_x1 = dlogit * head_ref[:, a:a + step]
        d_x0 = d_x1 * (cross[:, a:a + step] + 1.0) + lax.dot_general(
            d_low, down[a:a + step, :], NT, preferred_element_type=F32
        )
        d_x0 = d_x0.astype(BF16)
        for b in range(0, step, width):
            t = (a + b) // width - 1
            if t < 0:
                dg_ref[...] = d_x0[:, b:b + width]
            else:
                d_pool[t * 128:(t + 1) * 128, :] = d_x0[:, b:b + width]

    def grad_chunk(j):
        chunk_acc[...] = jnp.zeros_like(chunk_acc)

        def some(t):
            rows = pl.ds(pl.multiple_of(t * 256, 256), 256)
            pick = jnp.concatenate(
                [
                    hot(iota((chunk, 128), 0) == pos_row[pl.ds(t * 2 + h, 1), :] - j * chunk)
                    for h in range(2)
                ],
                axis=1,
            )
            chunk_acc[...] += jnp.dot(pick, d_pool[rows, :], preferred_element_type=F32)

        loop(0, tables // 2, some)
        grad_s[pl.ds(pl.multiple_of(j * chunk, 16), chunk), :] = chunk_acc[...].astype(BF16)

        def send(i):
            k = j * ring + i

            @pl.when(k != 0)
            def _():
                grad_copy(k).start()

        loop(0, ring, send)

        @pl.when(j == 0)
        def _():
            grad_r[0:slots, :] = grad_s[0:slots, :]

    def row_chunk(j):
        def one(i):
            k = j * ring + i

            @pl.when(k != 0)
            def _():
                grad_copy(k).wait_recv()

        loop(0, ring, one)
        part = pl.ds(pl.multiple_of(j * chunk, 16), chunk)
        turned = grad_r[part, :].astype(F32).T.astype(BF16)
        for b in range(groups):
            acc[b] += jnp.dot(
                turned, counts[part, b * block:(b + 1) * block], preferred_element_type=F32
            )

    def backward(j):
        grad_chunk(j)

        @pl.when(j >= LAG)
        def _():
            row_chunk(j - LAG)

    loop(0, ring, backward)
    h_step1()
    h_step2()
    loop(ring - LAG, ring, row_chunk)

    def pr_copy(d):
        r = lax.rem(y + d, pairs)
        return remote(acc.at[(1 - c) * pairs + r], pair_r.at[r], pr_ss.at[d], pr_rs.at[d], mate)

    def rs_copy(d):
        return remote(pair_r.at[lax.rem(y + d, pairs)], rs_r.at[d], rs_ss.at[d], rs_rs.at[d], along_y(d))

    def out_block(side, r):
        return rg_ref.at[pl.ds(pl.multiple_of((side * pairs + r) * block, block), block)]

    def ag_copy(d):
        here = out_block(c, y)
        return remote(here, here, ag_ss.at[d], ag_rs.at[d], along_y(d))

    def pa_copy(d):
        here = out_block(c, lax.rem(y + pairs - d, pairs))
        return remote(here, here, pa_ss.at[d], pa_rs.at[d], mate)

    loop(0, pairs, lambda d: pr_copy(lax.rem(d + 1, pairs)).start())

    def pair_sum(n):
        d = lax.rem(n + 1, pairs)
        pr_copy(d).wait_recv()
        r = lax.rem(y + d, pairs)
        pair_r[r] = pair_r[r] + acc[c * pairs + r]

        @pl.when(d != 0)
        def _():
            rs_copy(d).start()

    loop(0, pairs, pair_sum)
    h_step3()
    loop(1, pairs, lambda d: rs_copy(d).wait_recv())
    total = pair_r[y]
    for d in range(1, pairs):
        total = total + rs_r[d]
    rg_ref[pl.ds(pl.multiple_of((c * pairs + y) * block, block), block), :] = total.T
    loop(1, pairs, lambda d: ag_copy(d).start())
    pa_copy(0).start()
    h_step4()

    def forward_block(d):
        ag_copy(d).wait_recv()
        pa_copy(d).start()

    loop(1, pairs, forward_block)
    loop(0, pairs, lambda d: pa_copy(d).wait_recv())
    loop(1, ring, lambda d: h5_copy(d).wait_recv())

    def sent(k):
        code_copy(k).wait_send()
        pool_copy(k).wait_send()
        grad_copy(k).wait_send()

    loop(1, peers, sent)

    def sent_x(d):
        h1_copy(d).wait_send()
        h2_copy(d).wait_send()
        h5_copy(d).wait_send()

    loop(1, ring, sent_x)

    def sent_y(d):
        h3_copy(d).wait_send()
        rs_copy(d).wait_send()
        ag_copy(d).wait_send()

    loop(1, pairs, sent_y)

    def sent_pair(d):
        pr_copy(d).wait_send()
        pa_copy(d).wait_send()

    loop(0, pairs, sent_pair)
    h4_copy().wait_send()


def body(
    table_window, dense_part, bag_rows, bag_lengths, bag_owner, labels, sample_weight, down_w, up_w, cross_bias, head_w
):
    peers = lax.axis_size("emb")
    groups = lax.axis_size("grp")
    ring = 1
    while ring * ring < peers:
        ring *= 2
    pairs = groups // 2
    samples, width = dense_part.shape
    tables, entries = bag_rows.shape[1:]
    local_rows = table_window.shape[0]
    cross_width, rank = down_w.shape
    capacity = samples * tables * 3 // (2 * peers)
    slots = -(-capacity // 16) * 16
    chunk = ring * slots
    bags = samples * tables
    block = local_rows // groups
    tiles = cross_width // width
    own = bag_owner.reshape(samples, tables).T
    lengths = bag_lengths.T
    rows = bag_rows.transpose(1, 2, 0).reshape(tables * entries, samples)
    vmem = pl.BlockSpec(memory_space=pltpu.VMEM)
    hbm = pl.BlockSpec(memory_space=pl.ANY)
    dma = pltpu.SemaphoreType.DMA
    row_grad, sums, dense_grad = pl.pallas_call(
        functools.partial(kernel, ring, tables, slots, pairs),
        out_shape=(
            jax.ShapeDtypeStruct((local_rows, width), F32),
            jax.ShapeDtypeStruct((ring * 8, width), F32),
            jax.ShapeDtypeStruct((samples, width), BF16),
        ),
        in_specs=[vmem] * 9 + [hbm] * 2,
        out_specs=(vmem, vmem, vmem),
        scratch_shapes=[
            pltpu.VMEM((cross_width, rank), BF16),
            pltpu.VMEM((rank, cross_width), BF16),
            pltpu.VMEM((-(-tables // 8) * 8, 128), I32),
            pltpu.VMEM((bags, 128), I32),
            pltpu.VMEM((2 * slots * 8, 128), F32),
            pltpu.VMEM((peers * 8, 128), I32),
            pltpu.VMEM((peers * 8, 128), I32),
            pltpu.VMEM((peers * slots, local_rows), BF16),
            pltpu.VMEM((peers * slots, width), BF16),
            pltpu.VMEM((peers * slots, width), BF16),
            pltpu.VMEM((peers * slots, width), BF16),
            pltpu.VMEM((peers * slots, width), BF16),
            pltpu.VMEM((samples, cross_width), BF16),
            pltpu.VMEM((bags, width), F32),
            pltpu.VMEM((samples, cross_width), F32),
            pltpu.VMEM((bags, width), BF16),
            pltpu.VMEM((chunk, width), F32),
            pltpu.VMEM((groups, width, block), F32),
            pltpu.VMEM((pairs, width, block), F32),
            pltpu.VMEM((pairs, width, block), F32),
            pltpu.VMEM((ring * 8, 128), F32),
            pltpu.VMEM((ring * 8, 128), F32),
            pltpu.VMEM((ring * 8, 128), F32),
            pltpu.VMEM((pairs * 8, 128), F32),
            pltpu.VMEM((16, 128), F32),
            dma((2,)),
            dma((peers,)),
            dma((peers,)),
            dma((peers,)),
            dma((peers,)),
            dma((peers,)),
            dma((peers,)),
            dma((pairs,)),
            dma((pairs,)),
            dma((pairs,)),
            dma((pairs,)),
            dma((pairs,)),
            dma((pairs,)),
            dma((pairs,)),
            dma((pairs,)),
            dma((5, max(ring, pairs))),
            dma((5, max(ring, pairs))),
        ],
        compiler_params=pltpu.CompilerParams(
            collective_id=0, has_side_effects=True, vmem_limit_bytes=60 * 1024 * 1024
        ),
    )(
        own, lengths, rows, labels.reshape(1, samples), sample_weight.reshape(1, samples), dense_part, table_window,
        cross_bias.reshape(1, cross_width), head_w.reshape(1, cross_width), down_w, up_w,
    )
    head_grad = sums[:tiles].reshape(cross_width)
    bias_grad = sums[tiles:2 * tiles].reshape(cross_width)
    return row_grad, head_grad, bias_grad, dense_grad


def solution(mesh):
    in_specs = (
        P("emb", None),
        P(("grp", "emb"), None),
        P(("grp", "emb"), None, None),
        P(("grp", "emb"), None),
        P(("grp", "emb"), None, None),
        P(("grp", "emb")),
        P(("grp", "emb")),
        P(),
        P(),
        P(),
        P(),
    )
    out_specs = (P("emb", None), P(), P(), P(("grp", "emb"), None))
    return jax.shard_map(body, mesh=mesh, in_specs=in_specs, out_specs=out_specs, check_vma=False)
```

```python
import functools

import jax
import jax.numpy as jnp
from jax import lax
from jax.experimental import pallas as pl
from jax.experimental.pallas import tpu as pltpu
from jax.sharding import PartitionSpec as P

MESH = pl.DeviceIdType.MESH
F32 = jnp.float32
BF16 = jnp.bfloat16
I32 = jnp.int32
I16 = jnp.int16
NT = (((1,), (1,)), ((), ()))
LAG = 3
UNROLL = 4


def iota(shape, dim):
    return lax.broadcasted_iota(I32, shape, dim)


def hot(mask):
    return jnp.where(mask, jnp.ones((), BF16), jnp.zeros((), BF16))


def wide(row):
    return jnp.broadcast_to(row, (16, row.shape[1])).astype(I16)


def hot_rows(index, row):
    rows, lanes = index.shape[0], row.shape[1]
    parts = []
    for a in range(0, lanes, 128):
        parts.append(hot(index.reshape(rows // 16, 16, 128) == wide(row[:, a:a + 128])[None]).reshape(rows, 128))
    return jnp.concatenate(parts, axis=1) if len(parts) > 1 else parts[0]


def kernel(
    ring, tables, slots, pairs,
    own_ref, len_ref, rows_ref, label_ref, weight_ref, dense_ref, table_ref, bias_ref, head_ref,
    down_any, up_any,
    rg_ref, hb_ref, dg_ref,
    down, up, pos_row, slot_row, pos_col, owners, pick, turned_pick, req_acc, code_s, code_r, counts, pool_s, pool_r, grad_s, grad_r,
    x0, x0_acc, cross, d_pool, acc, pair_r, rs_r,
    hb, h1, h2, h3, h4,
    w_sem, code_ss, code_rs, pool_ss, pool_rs, grad_ss, grad_rs,
    pr_ss, pr_rs, rs_ss, rs_rs, ag_ss, ag_rs, pa_ss, pa_rs, h_ss, h_rs,
):
    peers = ring * ring
    groups = 2 * pairs
    chunk = ring * slots
    bits = ring.bit_length() - 1
    code_rows = slots * 8 // 128
    local_rows, width = table_ref.shape
    block = local_rows // groups
    tiles = tables + 1
    me = lax.axis_index("emb")
    grp = lax.axis_index("grp")
    x, z = me // ring, lax.rem(me, ring)
    y, c = grp // 2, lax.rem(grp, 2)
    mate = {"grp": grp + 1 - 2 * c}

    def ahead(k):
        dx = lax.rem(k, ring)
        dz = lax.rem(dx + k // ring, ring)
        return {"emb": lax.rem(x + dx, ring) * ring + lax.rem(z + dz, ring)}

    def behind(k):
        dx = lax.rem(k, ring)
        dz = lax.rem(dx + k // ring, ring)
        return {"emb": lax.rem(x + ring - dx, ring) * ring + lax.rem(z + ring - dz, ring)}

    def along_x(d):
        return {"emb": lax.rem(x + d, ring) * ring + z}

    def along_z(d):
        return {"emb": x * ring + lax.rem(z + d, ring)}

    def along_y(d):
        return {"grp": lax.rem(y + d, pairs) * 2 + c}

    def remote(src, dst, send, recv, where):
        return pltpu.make_async_remote_copy(
            src_ref=src, dst_ref=dst, send_sem=send, recv_sem=recv, device_id=where, device_id_type=MESH
        )

    def loop(low, high, step):
        def run(i, carry):
            step(i)
            return carry

        lax.fori_loop(low, high, run, 0)

    down_copy = pltpu.make_async_copy(down_any, down, w_sem.at[0])
    up_copy = pltpu.make_async_copy(up_any, up, w_sem.at[1])
    down_copy.start()
    up_copy.start()

    barrier = pltpu.get_barrier_semaphore()
    loop(1, peers, lambda k: pl.semaphore_signal(barrier, inc=1, device_id=ahead(k), device_id_type=MESH))
    loop(1, pairs, lambda d: pl.semaphore_signal(barrier, inc=1, device_id=along_y(d), device_id_type=MESH))
    pl.semaphore_signal(barrier, inc=1, device_id=mate, device_id_type=MESH)

    number = iota((max(chunk, 256), 128), 0).astype(I16)
    lane = iota((16, 128), 1).astype(I16)
    upper = jnp.concatenate(
        [
            jnp.where(iota((128, 128), 0) < iota((128, 128), 1), 1.0, 0.0).astype(BF16),
            jnp.ones((128, 128), BF16),
        ],
        axis=1,
    )
    half = tables // 2
    names = slots * 8

    def bucket(t, carry):
        owner = own_ref[pl.ds(t, 1), :]
        dx = ((owner >> bits) - x) & (ring - 1)
        dz = ((owner & (ring - 1)) - z) & (ring - 1)
        kind = ((dz - dx) & (ring - 1)) * ring + dx
        mine = jnp.where(iota((128, 128), 0) == kind, 1.0, 0.0)
        mine_b = mine.astype(BF16)
        owners[t // half, :, pl.ds(pl.multiple_of(lax.rem(t, half) * 128, 128), 128)] = mine_b
        sums = jnp.dot(mine_b, upper, preferred_element_type=F32)
        slot = jnp.sum(mine * (sums[:, :128] + carry), axis=0, keepdims=True).astype(I32)
        pos_row[pl.ds(t, 1), :] = kind * slots + slot
        slot_row[pl.ds(t, 1), :] = slot
        return carry + sums[:, 128:]

    lax.fori_loop(0, tables, bucket, jnp.zeros((128, 128), F32), unroll=2)

    def spread(t):
        slot = slot_row[pl.ds(t, 1), :]
        live = iota((8, 128), 0) < len_ref[pl.ds(t, 1), :]
        code = jnp.where(live, rows_ref[pl.ds(pl.multiple_of(t * 8, 8), 8), :] + 1, 0)
        here = iota((slots, 8, 128), 0) == slot[None]
        top = pl.multiple_of((t // half) * 2 * names, 16)
        lanes = pl.ds(pl.multiple_of(lax.rem(t, half) * 128, 128), 128)
        for part, at in ((code >> 4, 0), (code & 15, names)):
            value = jnp.where(here, part.astype(F32)[None], 0.0).reshape(names, 128).astype(BF16)
            counts[pl.ds(top + at, names), lanes] = value

    loop(0, tables, spread)
    req = lax.dot_general(counts[0:2 * names, 0:half * 128], owners[0], NT, preferred_element_type=F32)
    req_acc[...] = req
    req = lax.dot_general(counts[2 * names:4 * names, 0:half * 128], owners[1], NT, preferred_element_type=F32)
    req_acc[...] += req
    for p in range(code_rows):
        high = req_acc[p * 128:(p + 1) * 128, :]
        low = req_acc[names + p * 128:names + (p + 1) * 128, :]
        tile = (high * 16.0 + low - 1.0).T
        code_s[pl.ds(p, peers, stride=8), :] = tile[:peers].astype(I32)

    pl.semaphore_wait(barrier, peers - 1 + pairs - 1 + 1)

    def code_copy(k):
        part = pl.ds(pl.multiple_of(k * 8, 8), 8)
        return remote(code_s.at[part], code_r.at[part], code_ss.at[k], code_rs.at[k], ahead(k))

    def pool_copy(k):
        part = pl.ds(pl.multiple_of(k * slots, 16), slots)
        return remote(pool_s.at[part], pool_r.at[part], pool_ss.at[k], pool_rs.at[k], behind(k))

    def grad_copy(k):
        part = pl.ds(pl.multiple_of(k * slots, 16), slots)
        return remote(grad_s.at[part], grad_r.at[part], grad_ss.at[k], grad_rs.at[k], ahead(k))

    loop(1, peers, lambda k: code_copy(k).start())
    code_r[0:8, :] = code_s[0:8, :]

    def turn(t):
        row = jnp.broadcast_to(pos_row[pl.ds(t, 1), :], (128, 128)).astype(F32)
        pos_col[pl.ds(pl.multiple_of(t * 128, 128), 128), :] = row.T.astype(I32).astype(I16)
        x0_acc[pl.ds(pl.multiple_of(t * 128, 128), 128), :] = jnp.zeros((128, 128), F32)

    loop(0, tables, turn)
    acc[...] = jnp.zeros_like(acc)

    def count_bags(k):
        tile = code_r[pl.ds(pl.multiple_of(k * 8, 8), 8), :]
        base = pl.multiple_of(k * slots, 16)
        for first in range(0, code_rows, 2):
            last = min(first + 2, code_rows)
            code = jnp.concatenate([tile[p:p + 1, :] for p in range(first, last)], axis=1)
            bags = (last - first) * 16
            lanes = bags * 8
            spans = local_rows // 256
            key = (code >> 8) * bags + (iota((1, lanes), 1) >> 3)
            left = hot_rows(number[:spans * bags], key)
            right = hot_rows(number[:256], code & 255)
            out = lax.dot_general(left, right, NT, preferred_element_type=F32).astype(BF16)
            for s in range(spans):
                counts[pl.ds(base + first * 16, bags), s * 256:(s + 1) * 256] = out[s * bags:(s + 1) * bags, :]

    def pool_chunk(j):
        def one(n):
            first = j * ring + n * UNROLL

            @pl.when(first != 0)
            def _():
                code_copy(first).wait_recv()

            for i in range(1, UNROLL):
                code_copy(first + i).wait_recv()
            for i in range(UNROLL):
                count_bags(first + i)

        loop(0, ring // UNROLL, one)
        part = pl.ds(pl.multiple_of(j * chunk, 16), chunk)
        pool_s[part, :] = jnp.dot(counts[part, :], table_ref[...], preferred_element_type=F32).astype(BF16)

        def send(i):
            k = j * ring + i

            @pl.when(k != 0)
            def _():
                pool_copy(k).start()

        loop(0, ring, send)

        @pl.when(j == 0)
        def _():
            pool_r[0:slots, :] = pool_s[0:slots, :]

    def place_pair(j):
        def one(i):
            k = j * 2 * ring + i

            @pl.when(k != 0)
            def _():
                pool_copy(k).wait_recv()

        loop(0, 2 * ring, one)
        base = pl.multiple_of(j * 2 * chunk, 16)
        offset = base.astype(I16)

        def some(t):
            rows = pl.ds(pl.multiple_of(t * 256, 256), 256)
            column = (pos_col[rows, :] - offset).reshape(16, 16, 128)
            column = jnp.where(column >= chunk, column - chunk, column)
            for q in range(0, chunk, 128):
                pick[rows, q:q + 128] = hot(column == (lane + q)[None]).reshape(256, 128)

        loop(0, tables // 2, some)
        right = jnp.concatenate([pool_r[pl.ds(base, chunk), :], pool_r[pl.ds(base + chunk, chunk), :]], axis=1)

        def apply(n):
            rows = pl.ds(pl.multiple_of(n * half * 128, 128), half * 128)
            out = jnp.dot(pick[rows, :], right, preferred_element_type=F32)
            first = pos_col[rows, :].astype(I32) < base + chunk
            x0_acc[rows, :] += jnp.where(first, out[:, :width], out[:, width:])

        loop(0, 2, apply)

    def forward(j):
        pool_chunk(j)
        if ring >= 8:

            @pl.when((j >= 5) & (lax.rem(j, 2) == 1))
            def _():
                place_pair((j - 5) // 2)

    loop(0, ring, forward)
    loop(ring // 2 - 2 if ring >= 8 else 0, ring // 2, place_pair)

    down_copy.wait()
    up_copy.wait()
    x0[:, :width] = dense_ref[...]
    for t in range(tables):
        x0[:, (t + 1) * width:(t + 2) * width] = x0_acc[t * 128:(t + 1) * 128, :].astype(BF16)
    step = 3 * width
    cuts = range(0, tiles * width, step)
    low = jnp.dot(x0[...], down[...], preferred_element_type=F32).astype(BF16)
    logit_acc = jnp.zeros((128, width), F32)
    for a in cuts:
        part = jnp.dot(low, up[:, a:a + step], preferred_element_type=F32) + bias_ref[a:a + step].reshape(1, step)
        cross[:, a:a + step] = part
        x0f = x0[:, a:a + step].astype(F32)
        term = (x0f * part + x0f) * head_ref[a:a + step].reshape(1, step)
        for b in range(0, step, width):
            logit_acc = logit_acc + term[:, b:b + width]
    logit = jnp.sum(logit_acc, axis=1, keepdims=True)
    label = jnp.broadcast_to(label_ref[...].astype(F32), (128, 128)).T[:, 0:1]
    weight = jnp.broadcast_to(weight_ref[...], (128, 128)).T[:, 0:1]
    dlogit = weight * (jax.nn.sigmoid(logit) - label)
    hb[...] = jnp.zeros_like(hb)
    for a in cuts:
        x0f = x0[:, a:a + step].astype(F32)
        x1 = x0f * cross[:, a:a + step] + x0f
        d_cross = dlogit * head_ref[a:a + step].reshape(1, step) * x0f
        head_part = jnp.sum(dlogit * x1, axis=0, keepdims=True)
        bias_part = jnp.sum(d_cross, axis=0, keepdims=True)
        for b in range(0, step, width):
            r = (a + b) // width
            hb[r:r + 1, :] = head_part[:, b:b + width]
            hb[tiles + r:tiles + r + 1, :] = bias_part[:, b:b + width]
        x0[:, a:a + step] = d_cross.astype(BF16)
    d_low = lax.dot_general(x0[...], up[...], NT, preferred_element_type=F32).astype(BF16)

    def h_part(r):
        return pl.ds(pl.multiple_of(r * 8, 8), 8)

    def h1_copy(d):
        return remote(hb.at[h_part(lax.rem(x + d, ring))], h1.at[h_part(d)], h_ss.at[0, d], h_rs.at[0, d], along_x(d))

    def h2_copy(d):
        return remote(h2.at[h_part(z)], h2.at[h_part(z)], h_ss.at[1, d], h_rs.at[1, d], along_z(d))

    def h3_copy(d):
        return remote(h3.at[h_part(y)], h3.at[h_part(y)], h_ss.at[2, d], h_rs.at[2, d], along_y(d))

    def h4_copy():
        return remote(h4.at[h_part(c)], h4.at[h_part(c)], h_ss.at[3, 0], h_rs.at[3, 0], mate)

    def h5_copy(d):
        return remote(hb_ref.at[h_part(x)], hb_ref.at[h_part(x)], h_ss.at[4, d], h_rs.at[4, d], along_x(d))

    loop(1, ring, lambda d: h1_copy(d).start())

    def total_of(ref, count, start=0):
        total = ref[start * 8:start * 8 + 8, :]
        for r in range(start + 1, count):
            total = total + ref[r * 8:r * 8 + 8, :]
        return total

    def h_step1():
        loop(1, ring, lambda d: h1_copy(d).wait_recv())
        h2[h_part(z), :] = total_of(h1, ring, 1) + hb[h_part(x), :]
        loop(1, ring, lambda d: h2_copy(d).start())

    def h_step2():
        loop(1, ring, lambda d: h2_copy(d).wait_recv())
        h3[h_part(y), :] = total_of(h2, ring)
        loop(1, pairs, lambda d: h3_copy(d).start())

    def h_step3():
        loop(1, pairs, lambda d: h3_copy(d).wait_recv())
        h4[h_part(c), :] = total_of(h3, pairs)
        h4_copy().start()

    def h_step4():
        h4_copy().wait_recv()
        hb_ref[h_part(x), :] = total_of(h4, 2)
        loop(1, ring, lambda d: h5_copy(d).start())

    for a in cuts:
        d_x1 = dlogit * head_ref[a:a + step].reshape(1, step)
        d_x0 = d_x1 * (cross[:, a:a + step] + 1.0) + lax.dot_general(
            d_low, down[a:a + step, :], NT, preferred_element_type=F32
        )
        d_x0 = d_x0.astype(BF16)
        for b in range(0, step, width):
            t = (a + b) // width - 1
            if t < 0:
                dg_ref[...] = d_x0[:, b:b + width]
            else:
                d_pool[t * 128:(t + 1) * 128, :] = d_x0[:, b:b + width]

    def grad_chunk(j):
        def some(t):
            for h in range(2):
                lanes = pl.ds(pl.multiple_of(t * 256 + h * 128, 128), 128)
                turned_pick[:, lanes] = hot_rows(number[:chunk], pos_row[pl.ds(t * 2 + h, 1), :] - j * chunk)

        loop(0, tables // 2, some)
        out = jnp.dot(turned_pick[...], d_pool[...], preferred_element_type=F32)
        grad_s[pl.ds(pl.multiple_of(j * chunk, 16), chunk), :] = out.astype(BF16)

        def send(i):
            k = j * ring + i

            @pl.when(k != 0)
            def _():
                grad_copy(k).start()

        loop(0, ring, send)

        @pl.when(j == 0)
        def _():
            grad_r[0:slots, :] = grad_s[0:slots, :]

    def row_chunk(j):
        def one(i):
            k = j * ring + i

            @pl.when(k != 0)
            def _():
                grad_copy(k).wait_recv()

        loop(0, ring, one)
        part = pl.ds(pl.multiple_of(j * chunk, 16), chunk)
        turned = grad_r[part, :].astype(F32).T.astype(BF16)
        for b in range(0, local_rows, 256):
            out = jnp.dot(turned, counts[part, b:b + 256], preferred_element_type=F32)
            for a in range(0, 256, 128):
                g, at = (a + b) // block, (a + b) % block
                acc[g, :, at:at + 128] += out[:, a:a + 128]

    def backward(j):
        grad_chunk(j)

        @pl.when(j >= LAG)
        def _():
            row_chunk(j - LAG)

    loop(0, ring, backward)
    h_step1()
    h_step2()
    loop(ring - LAG, ring, row_chunk)

    def pr_copy(d):
        r = lax.rem(y + d, pairs)
        return remote(acc.at[(1 - c) * pairs + r], pair_r.at[r], pr_ss.at[d], pr_rs.at[d], mate)

    def rs_copy(d):
        return remote(pair_r.at[lax.rem(y + d, pairs)], rs_r.at[d], rs_ss.at[d], rs_rs.at[d], along_y(d))

    def out_block(side, r):
        return rg_ref.at[pl.ds(pl.multiple_of((side * pairs + r) * block, block), block)]

    def ag_copy(d):
        here = out_block(c, y)
        return remote(here, here, ag_ss.at[d], ag_rs.at[d], along_y(d))

    def pa_copy(d):
        here = out_block(c, lax.rem(y + pairs - d, pairs))
        return remote(here, here, pa_ss.at[d], pa_rs.at[d], mate)

    loop(0, pairs, lambda d: pr_copy(lax.rem(d + 1, pairs)).start())

    def pair_sum(n):
        d = lax.rem(n + 1, pairs)
        pr_copy(d).wait_recv()
        r = lax.rem(y + d, pairs)
        pair_r[r] = pair_r[r] + acc[c * pairs + r]

        @pl.when(d != 0)
        def _():
            rs_copy(d).start()

    loop(0, pairs, pair_sum)
    h_step3()
    loop(1, pairs, lambda d: rs_copy(d).wait_recv())
    total = pair_r[y]
    for d in range(1, pairs):
        total = total + rs_r[d]
    rg_ref[pl.ds(pl.multiple_of((c * pairs + y) * block, block), block), :] = total.T
    loop(1, pairs, lambda d: ag_copy(d).start())
    pa_copy(0).start()
    h_step4()

    def forward_block(d):
        ag_copy(d).wait_recv()
        pa_copy(d).start()

    loop(1, pairs, forward_block)
    loop(0, pairs, lambda d: pa_copy(d).wait_recv())
    loop(1, ring, lambda d: h5_copy(d).wait_recv())

    def sent(k):
        code_copy(k).wait_send()
        pool_copy(k).wait_send()
        grad_copy(k).wait_send()

    loop(1, peers, sent)

    def sent_x(d):
        h1_copy(d).wait_send()
        h2_copy(d).wait_send()
        h5_copy(d).wait_send()

    loop(1, ring, sent_x)

    def sent_y(d):
        h3_copy(d).wait_send()
        rs_copy(d).wait_send()
        ag_copy(d).wait_send()

    loop(1, pairs, sent_y)

    def sent_pair(d):
        pr_copy(d).wait_send()
        pa_copy(d).wait_send()

    loop(0, pairs, sent_pair)
    h4_copy().wait_send()


def body(
    table_window, dense_part, bag_rows, bag_lengths, bag_owner, labels, sample_weight, down_w, up_w, cross_bias, head_w
):
    peers = lax.axis_size("emb")
    groups = lax.axis_size("grp")
    ring = 1
    while ring * ring < peers:
        ring *= 2
    pairs = groups // 2
    samples, width = dense_part.shape
    tables, entries = bag_rows.shape[1:]
    local_rows = table_window.shape[0]
    cross_width, rank = down_w.shape
    capacity = samples * tables * 3 // (2 * peers)
    slots = -(-capacity // 16) * 16
    chunk = ring * slots
    bags = samples * tables
    block = local_rows // groups
    tiles = cross_width // width
    own = bag_owner.reshape(samples, tables).T
    lengths = bag_lengths.T
    rows = bag_rows.transpose(1, 2, 0).reshape(tables * entries, samples)
    vmem = pl.BlockSpec(memory_space=pltpu.VMEM)
    hbm = pl.BlockSpec(memory_space=pl.ANY)
    dma = pltpu.SemaphoreType.DMA
    row_grad, sums, dense_grad = pl.pallas_call(
        functools.partial(kernel, ring, tables, slots, pairs),
        out_shape=(
            jax.ShapeDtypeStruct((local_rows, width), F32),
            jax.ShapeDtypeStruct((ring * 8, width), F32),
            jax.ShapeDtypeStruct((samples, width), BF16),
        ),
        in_specs=[vmem] * 9 + [hbm] * 2,
        out_specs=(vmem, vmem, vmem),
        scratch_shapes=[
            pltpu.VMEM((cross_width, rank), BF16),
            pltpu.VMEM((rank, cross_width), BF16),
            pltpu.VMEM((-(-tables // 8) * 8, 128), I32),
            pltpu.VMEM((-(-tables // 8) * 8, 128), I32),
            pltpu.VMEM((bags, 128), I16),
            pltpu.VMEM((2, 128, bags // 2), BF16),
            pltpu.VMEM((bags, chunk), BF16),
            pltpu.VMEM((chunk, bags), BF16),
            pltpu.VMEM((2 * slots * 8, 128), F32),
            pltpu.VMEM((peers * 8, 128), I32),
            pltpu.VMEM((peers * 8, 128), I32),
            pltpu.VMEM((max(peers, 32) * slots, local_rows), BF16),
            pltpu.VMEM((peers * slots, width), BF16),
            pltpu.VMEM((peers * slots, width), BF16),
            pltpu.VMEM((peers * slots, width), BF16),
            pltpu.VMEM((peers * slots, width), BF16),
            pltpu.VMEM((samples, cross_width), BF16),
            pltpu.VMEM((bags, width), F32),
            pltpu.VMEM((samples, cross_width), F32),
            pltpu.VMEM((bags, width), BF16),
            pltpu.VMEM((groups, width, block), F32),
            pltpu.VMEM((pairs, width, block), F32),
            pltpu.VMEM((pairs, width, block), F32),
            pltpu.VMEM((ring * 8, 128), F32),
            pltpu.VMEM((ring * 8, 128), F32),
            pltpu.VMEM((ring * 8, 128), F32),
            pltpu.VMEM((pairs * 8, 128), F32),
            pltpu.VMEM((16, 128), F32),
            dma((2,)),
            dma((peers,)),
            dma((peers,)),
            dma((peers,)),
            dma((peers,)),
            dma((peers,)),
            dma((peers,)),
            dma((pairs,)),
            dma((pairs,)),
            dma((pairs,)),
            dma((pairs,)),
            dma((pairs,)),
            dma((pairs,)),
            dma((pairs,)),
            dma((pairs,)),
            dma((5, max(ring, pairs))),
            dma((5, max(ring, pairs))),
        ],
        compiler_params=pltpu.CompilerParams(
            collective_id=0, has_side_effects=True, vmem_limit_bytes=60 * 1024 * 1024
        ),
    )(
        own, lengths, rows, labels.reshape(1, samples), sample_weight.reshape(1, samples), dense_part, table_window,
        cross_bias, head_w, down_w, up_w,
    )
    head_grad = sums[:tiles].reshape(cross_width)
    bias_grad = sums[tiles:2 * tiles].reshape(cross_width)
    return row_grad, head_grad, bias_grad, dense_grad


def solution(mesh):
    in_specs = (
        P("emb", None),
        P(("grp", "emb"), None),
        P(("grp", "emb"), None, None),
        P(("grp", "emb"), None),
        P(("grp", "emb"), None, None),
        P(("grp", "emb")),
        P(("grp", "emb")),
        P(),
        P(),
        P(),
        P(),
    )
    out_specs = (P("emb", None), P(), P(), P(("grp", "emb"), None))
    return jax.shard_map(body, mesh=mesh, in_specs=in_specs, out_specs=out_specs, check_vma=False)
```

```python
import functools

import jax
import jax.numpy as jnp
from jax import lax
from jax.experimental import pallas as pl
from jax.experimental.pallas import tpu as pltpu
from jax.sharding import PartitionSpec as P

MESH = pl.DeviceIdType.MESH
F32 = jnp.float32
BF16 = jnp.bfloat16
I32 = jnp.int32
I16 = jnp.int16
NT = (((1,), (1,)), ((), ()))
LAG = 3
UNROLL = 4


def iota(shape, dim):
    return lax.broadcasted_iota(I32, shape, dim)


def hot(mask):
    return jnp.where(mask, jnp.ones((), BF16), jnp.zeros((), BF16))


def wide(row):
    return jnp.broadcast_to(row, (16, row.shape[1])).astype(I16)


def hot_rows(index, row):
    rows, lanes = index.shape[0], row.shape[1]
    parts = []
    for a in range(0, lanes, 128):
        parts.append(hot(index.reshape(rows // 16, 16, 128) == wide(row[:, a:a + 128])[None]).reshape(rows, 128))
    return jnp.concatenate(parts, axis=1) if len(parts) > 1 else parts[0]


def kernel(
    ring, tables, slots, pairs,
    own_ref, len_ref, rows_ref, label_ref, weight_ref, dense_ref, table_ref, bias_ref, head_ref,
    down_any, up_any,
    rg_ref, hb_ref, dg_ref,
    down, up, pos_row, slot_row, pos_col, owners, pick, turned_pick, req_acc, code_s, code_r, counts, pool_s, pool_r, grad_s, grad_r,
    x0, x0_acc, cross, d_pool, acc, pair_r, rs_s, rs_r,
    hb, h1, h2, h3, h4,
    w_sem, code_ss, code_rs, pool_ss, pool_rs, grad_ss, grad_rs,
    pr_ss, pr_rs, rs_ss, rs_rs, ag_ss, ag_rs, pa_ss, pa_rs, h_ss, h_rs,
):
    peers = ring * ring
    groups = 2 * pairs
    chunk = ring * slots
    bits = ring.bit_length() - 1
    code_rows = slots * 8 // 128
    local_rows, width = table_ref.shape
    block = local_rows // groups
    tiles = tables + 1
    me = lax.axis_index("emb")
    grp = lax.axis_index("grp")
    x, z = me // ring, lax.rem(me, ring)
    y, c = grp // 2, lax.rem(grp, 2)
    mate = {"grp": grp + 1 - 2 * c}

    def ahead(k):
        dx = lax.rem(k, ring)
        dz = lax.rem(dx + k // ring, ring)
        return {"emb": lax.rem(x + dx, ring) * ring + lax.rem(z + dz, ring)}

    def behind(k):
        dx = lax.rem(k, ring)
        dz = lax.rem(dx + k // ring, ring)
        return {"emb": lax.rem(x + ring - dx, ring) * ring + lax.rem(z + ring - dz, ring)}

    def along_x(d):
        return {"emb": lax.rem(x + d, ring) * ring + z}

    def along_z(d):
        return {"emb": x * ring + lax.rem(z + d, ring)}

    def along_y(d):
        return {"grp": lax.rem(y + d, pairs) * 2 + c}

    def remote(src, dst, send, recv, where):
        return pltpu.make_async_remote_copy(
            src_ref=src, dst_ref=dst, send_sem=send, recv_sem=recv, device_id=where, device_id_type=MESH
        )

    def loop(low, high, step):
        def run(i, carry):
            step(i)
            return carry

        lax.fori_loop(low, high, run, 0)

    down_copy = pltpu.make_async_copy(down_any, down, w_sem.at[0])
    up_copy = pltpu.make_async_copy(up_any, up, w_sem.at[1])
    down_copy.start()
    up_copy.start()

    barrier = pltpu.get_barrier_semaphore()
    loop(1, peers, lambda k: pl.semaphore_signal(barrier, inc=1, device_id=ahead(k), device_id_type=MESH))
    loop(1, pairs, lambda d: pl.semaphore_signal(barrier, inc=1, device_id=along_y(d), device_id_type=MESH))
    pl.semaphore_signal(barrier, inc=1, device_id=mate, device_id_type=MESH)

    number = iota((max(chunk, 256), 128), 0).astype(I16)
    lane = iota((16, 128), 1).astype(I16)
    upper = jnp.concatenate(
        [
            jnp.where(iota((128, 128), 0) < iota((128, 128), 1), 1.0, 0.0).astype(BF16),
            jnp.ones((128, 128), BF16),
        ],
        axis=1,
    )
    half = tables // 2
    names = slots * 8

    def bucket(t, carry):
        owner = own_ref[pl.ds(t, 1), :]
        dx = ((owner >> bits) - x) & (ring - 1)
        dz = ((owner & (ring - 1)) - z) & (ring - 1)
        kind = ((dz - dx) & (ring - 1)) * ring + dx
        mine = jnp.where(iota((128, 128), 0) == kind, 1.0, 0.0)
        mine_b = mine.astype(BF16)
        owners[t // half, :, pl.ds(pl.multiple_of(lax.rem(t, half) * 128, 128), 128)] = mine_b
        sums = jnp.dot(mine_b, upper, preferred_element_type=F32)
        slot = jnp.sum(mine * (sums[:, :128] + carry), axis=0, keepdims=True).astype(I32)
        pos_row[pl.ds(t, 1), :] = kind * slots + slot
        slot_row[pl.ds(t, 1), :] = slot
        return carry + sums[:, 128:]

    lax.fori_loop(0, tables, bucket, jnp.zeros((128, 128), F32), unroll=2)

    def spread(t):
        slot = slot_row[pl.ds(t, 1), :]
        live = iota((8, 128), 0) < len_ref[pl.ds(t, 1), :]
        code = jnp.where(live, rows_ref[pl.ds(pl.multiple_of(t * 8, 8), 8), :] + 1, 0)
        here = iota((slots, 8, 128), 0) == slot[None]
        top = pl.multiple_of((t // half) * 2 * names, 16)
        lanes = pl.ds(pl.multiple_of(lax.rem(t, half) * 128, 128), 128)
        for part, at in ((code >> 4, 0), (code & 15, names)):
            value = jnp.where(here, part.astype(F32)[None], 0.0).reshape(names, 128).astype(BF16)
            counts[pl.ds(top + at, names), lanes] = value

    loop(0, tables, spread)
    req = lax.dot_general(counts[0:2 * names, 0:half * 128], owners[0], NT, preferred_element_type=F32)
    req_acc[...] = req
    req = lax.dot_general(counts[2 * names:4 * names, 0:half * 128], owners[1], NT, preferred_element_type=F32)
    req_acc[...] += req
    for p in range(code_rows):
        high = req_acc[p * 128:(p + 1) * 128, :]
        low = req_acc[names + p * 128:names + (p + 1) * 128, :]
        tile = (high * 16.0 + low - 1.0).T
        code_s[pl.ds(p, peers, stride=8), :] = tile[:peers].astype(I32)

    pl.semaphore_wait(barrier, peers - 1 + pairs - 1 + 1)

    def code_copy(k):
        part = pl.ds(pl.multiple_of(k * 8, 8), code_rows)
        return remote(code_s.at[part], code_r.at[part], code_ss.at[k], code_rs.at[k], ahead(k))

    def pool_copy(k):
        part = pl.ds(pl.multiple_of(k * slots, 16), slots)
        return remote(pool_s.at[part], pool_r.at[part], pool_ss.at[k], pool_rs.at[k], behind(k))

    def grad_copy(k):
        part = pl.ds(pl.multiple_of(k * slots, 16), slots)
        return remote(grad_s.at[part], grad_r.at[part], grad_ss.at[k], grad_rs.at[k], ahead(k))

    loop(1, peers, lambda k: code_copy(k).start())
    code_r[0:8, :] = code_s[0:8, :]

    def turn(t):
        row = jnp.broadcast_to(pos_row[pl.ds(t, 1), :], (128, 128)).astype(F32)
        pos_col[pl.ds(pl.multiple_of(t * 128, 128), 128), :] = row.T.astype(I32).astype(I16)
        x0_acc[pl.ds(pl.multiple_of(t * 128, 128), 128), :] = jnp.zeros((128, 128), F32)


    def count_bags(k):
        tile = code_r[pl.ds(pl.multiple_of(k * 8, 8), 8), :]
        base = pl.multiple_of(k * slots, 16)
        for first in range(0, code_rows, 2):
            last = min(first + 2, code_rows)
            code = jnp.concatenate([tile[p:p + 1, :] for p in range(first, last)], axis=1)
            bags = (last - first) * 16
            lanes = bags * 8
            spans = local_rows // 256
            key = (code >> 8) * bags + (iota((1, lanes), 1) >> 3)
            left = hot_rows(number[:spans * bags], key)
            right = hot_rows(number[:256], code & 255)
            out = lax.dot_general(left, right, NT, preferred_element_type=F32).astype(BF16)
            for s in range(spans):
                counts[pl.ds(base + first * 16, bags), s * 256:(s + 1) * 256] = out[s * bags:(s + 1) * bags, :]

    def pool_chunk(j):
        def one(n):
            first = j * ring + n * UNROLL

            @pl.when(first != 0)
            def _():
                code_copy(first).wait_recv()

            for i in range(1, UNROLL):
                code_copy(first + i).wait_recv()
            for i in range(UNROLL):
                count_bags(first + i)

        loop(0, ring // UNROLL, one)
        part = pl.ds(pl.multiple_of(j * chunk, 16), chunk)
        pool_s[part, :] = jnp.dot(counts[part, :], table_ref[...], preferred_element_type=F32).astype(BF16)

        def send(i):
            k = j * ring + i

            @pl.when(k != 0)
            def _():
                pool_copy(k).start()

        loop(0, ring, send)

        @pl.when(j == 0)
        def _():
            pool_r[0:slots, :] = pool_s[0:slots, :]

    def place_pair(j):
        def one(i):
            k = j * 2 * ring + i

            @pl.when(k != 0)
            def _():
                pool_copy(k).wait_recv()

        loop(0, 2 * ring, one)
        base = pl.multiple_of(j * 2 * chunk, 16)
        offset = base.astype(I16)

        def some(t):
            rows = pl.ds(pl.multiple_of(t * 256, 256), 256)
            column = (pos_col[rows, :] - offset).reshape(16, 16, 128)
            column = jnp.where(column >= chunk, column - chunk, column)
            for q in range(0, chunk, 128):
                pick[rows, q:q + 128] = hot(column == (lane + q)[None]).reshape(256, 128)

        loop(0, tables // 2, some)
        right = jnp.concatenate([pool_r[pl.ds(base, chunk), :], pool_r[pl.ds(base + chunk, chunk), :]], axis=1)

        def apply(n):
            rows = pl.ds(pl.multiple_of(n * half * 128, 128), half * 128)
            out = jnp.dot(pick[rows, :], right, preferred_element_type=F32)
            first = pos_col[rows, :].astype(I32) < base + chunk
            x0_acc[rows, :] += jnp.where(first, out[:, :width], out[:, width:])

        loop(0, 2, apply)

    def forward(j):
        pool_chunk(j)

        @pl.when(j == 1)
        def _():
            loop(0, tables, turn)
            acc[...] = jnp.zeros_like(acc)

        if ring >= 8:

            @pl.when((j >= 5) & (lax.rem(j, 2) == 1))
            def _():
                place_pair((j - 5) // 2)

    loop(0, ring, forward)
    loop(ring // 2 - 2 if ring >= 8 else 0, ring // 2, place_pair)

    down_copy.wait()
    up_copy.wait()
    x0[:, :width] = dense_ref[...]
    for t in range(tables):
        x0[:, (t + 1) * width:(t + 2) * width] = x0_acc[t * 128:(t + 1) * 128, :].astype(BF16)
    step = 3 * width
    cuts = range(0, tiles * width, step)
    low = jnp.dot(x0[...], down[...], preferred_element_type=F32).astype(BF16)
    logit_acc = jnp.zeros((128, width), F32)
    for a in cuts:
        part = jnp.dot(low, up[:, a:a + step], preferred_element_type=F32) + bias_ref[a:a + step].reshape(1, step)
        cross[:, a:a + step] = part
        x0f = x0[:, a:a + step].astype(F32)
        term = (x0f * part + x0f) * head_ref[a:a + step].reshape(1, step)
        for b in range(0, step, width):
            logit_acc = logit_acc + term[:, b:b + width]
    logit = jnp.sum(logit_acc, axis=1, keepdims=True)
    label = jnp.broadcast_to(label_ref[...].astype(F32), (128, 128)).T[:, 0:1]
    weight = jnp.broadcast_to(weight_ref[...], (128, 128)).T[:, 0:1]
    dlogit = weight * (jax.nn.sigmoid(logit) - label)
    hb[...] = jnp.zeros_like(hb)
    for a in cuts:
        x0f = x0[:, a:a + step].astype(F32)
        x1 = x0f * cross[:, a:a + step] + x0f
        d_cross = dlogit * head_ref[a:a + step].reshape(1, step) * x0f
        head_part = jnp.sum(dlogit * x1, axis=0, keepdims=True)
        bias_part = jnp.sum(d_cross, axis=0, keepdims=True)
        for b in range(0, step, width):
            r = (a + b) // width
            hb[r:r + 1, :] = head_part[:, b:b + width]
            hb[tiles + r:tiles + r + 1, :] = bias_part[:, b:b + width]
        x0[:, a:a + step] = d_cross.astype(BF16)
    d_low = lax.dot_general(x0[...], up[...], NT, preferred_element_type=F32).astype(BF16)

    def h_part(r):
        return pl.ds(pl.multiple_of(r * 8, 8), 8)

    def h1_copy(d):
        return remote(hb.at[h_part(lax.rem(x + d, ring))], h1.at[h_part(d)], h_ss.at[0, d], h_rs.at[0, d], along_x(d))

    def h2_copy(d):
        return remote(h2.at[h_part(z)], h2.at[h_part(z)], h_ss.at[1, d], h_rs.at[1, d], along_z(d))

    def h3_copy(d):
        return remote(h3.at[h_part(y)], h3.at[h_part(y)], h_ss.at[2, d], h_rs.at[2, d], along_y(d))

    def h4_copy():
        return remote(h4.at[h_part(c)], h4.at[h_part(c)], h_ss.at[3, 0], h_rs.at[3, 0], mate)

    def h5_copy(d):
        return remote(hb_ref.at[h_part(x)], hb_ref.at[h_part(x)], h_ss.at[4, d], h_rs.at[4, d], along_x(d))

    loop(1, ring, lambda d: h1_copy(d).start())

    def total_of(ref, count, start=0):
        total = ref[start * 8:start * 8 + 8, :]
        for r in range(start + 1, count):
            total = total + ref[r * 8:r * 8 + 8, :]
        return total

    def h_step1():
        loop(1, ring, lambda d: h1_copy(d).wait_recv())
        h2[h_part(z), :] = total_of(h1, ring, 1) + hb[h_part(x), :]
        loop(1, ring, lambda d: h2_copy(d).start())

    def h_step2():
        loop(1, ring, lambda d: h2_copy(d).wait_recv())
        h3[h_part(y), :] = total_of(h2, ring)
        loop(1, pairs, lambda d: h3_copy(d).start())

    def h_step3():
        loop(1, pairs, lambda d: h3_copy(d).wait_recv())
        h4[h_part(c), :] = total_of(h3, pairs)
        h4_copy().start()

    def h_step4():
        h4_copy().wait_recv()
        hb_ref[h_part(x), :] = total_of(h4, 2)
        loop(1, ring, lambda d: h5_copy(d).start())

    for a in cuts:
        d_x1 = dlogit * head_ref[a:a + step].reshape(1, step)
        d_x0 = d_x1 * (cross[:, a:a + step] + 1.0) + lax.dot_general(
            d_low, down[a:a + step, :], NT, preferred_element_type=F32
        )
        d_x0 = d_x0.astype(BF16)
        for b in range(0, step, width):
            t = (a + b) // width - 1
            if t < 0:
                dg_ref[...] = d_x0[:, b:b + width]
            else:
                d_pool[t * 128:(t + 1) * 128, :] = d_x0[:, b:b + width]

    def grad_chunk(j):
        def some(t):
            for h in range(2):
                lanes = pl.ds(pl.multiple_of(t * 256 + h * 128, 128), 128)
                turned_pick[:, lanes] = hot_rows(number[:chunk], pos_row[pl.ds(t * 2 + h, 1), :] - j * chunk)

        loop(0, tables // 2, some)
        out = jnp.dot(turned_pick[...], d_pool[...], preferred_element_type=F32)
        grad_s[pl.ds(pl.multiple_of(j * chunk, 16), chunk), :] = out.astype(BF16)

        def send(i):
            k = j * ring + i

            @pl.when(k != 0)
            def _():
                grad_copy(k).start()

        loop(0, ring, send)

        @pl.when(j == 0)
        def _():
            grad_r[0:slots, :] = grad_s[0:slots, :]

    def row_chunk(j):
        def one(i):
            k = j * ring + i

            @pl.when(k != 0)
            def _():
                grad_copy(k).wait_recv()

        loop(0, ring, one)
        part = pl.ds(pl.multiple_of(j * chunk, 16), chunk)
        turned = grad_r[part, :].astype(F32).T.astype(BF16)
        for b in range(0, local_rows, 256):
            out = jnp.dot(turned, counts[part, b:b + 256], preferred_element_type=F32)
            for a in range(0, 256, 128):
                g, at = (a + b) // block, (a + b) % block
                acc[g, :, at:at + 128] += out[:, a:a + 128]

    def backward(j):
        grad_chunk(j)

        @pl.when(j >= LAG)
        def _():
            row_chunk(j - LAG)

    loop(0, ring, backward)
    h_step1()
    h_step2()
    loop(ring - LAG, ring, row_chunk)

    def pr_copy(d):
        r = lax.rem(y + d, pairs)
        return remote(acc.at[(1 - c) * pairs + r], pair_r.at[r], pr_ss.at[d], pr_rs.at[d], mate)

    def rs_copy(d):
        return remote(rs_s.at[lax.rem(y + d, pairs)], rs_r.at[d], rs_ss.at[d], rs_rs.at[d], along_y(d))

    def out_block(side, r):
        return rg_ref.at[pl.ds(pl.multiple_of((side * pairs + r) * block, block), block)]

    def ag_copy(d):
        here = out_block(c, y)
        return remote(here, here, ag_ss.at[d], ag_rs.at[d], along_y(d))

    def pa_copy(d):
        here = out_block(c, lax.rem(y + pairs - d, pairs))
        return remote(here, here, pa_ss.at[d], pa_rs.at[d], mate)

    loop(0, pairs, lambda d: pr_copy(lax.rem(d + 1, pairs)).start())

    def pair_sum(n):
        d = lax.rem(n + 1, pairs)
        pr_copy(d).wait_recv()
        r = lax.rem(y + d, pairs)
        both = pair_r[r] + acc[c * pairs + r]
        pair_r[r] = both
        rs_s[r] = both.astype(BF16)

        @pl.when(d != 0)
        def _():
            rs_copy(d).start()

    loop(0, pairs, pair_sum)
    h_step3()
    loop(1, pairs, lambda d: rs_copy(d).wait_recv())
    total = pair_r[y]
    for d in range(1, pairs):
        total = total + rs_r[d].astype(F32)
    rg_ref[pl.ds(pl.multiple_of((c * pairs + y) * block, block), block), :] = total.T.astype(BF16)
    loop(1, pairs, lambda d: ag_copy(d).start())
    pa_copy(0).start()
    h_step4()

    def forward_block(d):
        ag_copy(d).wait_recv()
        pa_copy(d).start()

    loop(1, pairs, forward_block)
    loop(0, pairs, lambda d: pa_copy(d).wait_recv())
    loop(1, ring, lambda d: h5_copy(d).wait_recv())

    def sent(k):
        code_copy(k).wait_send()
        pool_copy(k).wait_send()
        grad_copy(k).wait_send()

    loop(1, peers, sent)

    def sent_x(d):
        h1_copy(d).wait_send()
        h2_copy(d).wait_send()
        h5_copy(d).wait_send()

    loop(1, ring, sent_x)

    def sent_y(d):
        h3_copy(d).wait_send()
        rs_copy(d).wait_send()
        ag_copy(d).wait_send()

    loop(1, pairs, sent_y)

    def sent_pair(d):
        pr_copy(d).wait_send()
        pa_copy(d).wait_send()

    loop(0, pairs, sent_pair)
    h4_copy().wait_send()


def body(
    table_window, dense_part, bag_rows, bag_lengths, bag_owner, labels, sample_weight, down_w, up_w, cross_bias, head_w
):
    peers = lax.axis_size("emb")
    groups = lax.axis_size("grp")
    ring = 1
    while ring * ring < peers:
        ring *= 2
    pairs = groups // 2
    samples, width = dense_part.shape
    tables, entries = bag_rows.shape[1:]
    local_rows = table_window.shape[0]
    cross_width, rank = down_w.shape
    capacity = samples * tables * 3 // (2 * peers)
    slots = -(-capacity // 16) * 16
    chunk = ring * slots
    bags = samples * tables
    block = local_rows // groups
    tiles = cross_width // width
    own = bag_owner.reshape(samples, tables).T
    lengths = bag_lengths.T
    rows = bag_rows.transpose(1, 2, 0).reshape(tables * entries, samples)
    vmem = pl.BlockSpec(memory_space=pltpu.VMEM)
    hbm = pl.BlockSpec(memory_space=pl.ANY)
    dma = pltpu.SemaphoreType.DMA
    row_grad, sums, dense_grad = pl.pallas_call(
        functools.partial(kernel, ring, tables, slots, pairs),
        out_shape=(
            jax.ShapeDtypeStruct((local_rows, width), BF16),
            jax.ShapeDtypeStruct((ring * 8, width), F32),
            jax.ShapeDtypeStruct((samples, width), BF16),
        ),
        in_specs=[vmem] * 9 + [hbm] * 2,
        out_specs=(vmem, vmem, vmem),
        scratch_shapes=[
            pltpu.VMEM((cross_width, rank), BF16),
            pltpu.VMEM((rank, cross_width), BF16),
            pltpu.VMEM((-(-tables // 8) * 8, 128), I32),
            pltpu.VMEM((-(-tables // 8) * 8, 128), I32),
            pltpu.VMEM((bags, 128), I16),
            pltpu.VMEM((2, 128, bags // 2), BF16),
            pltpu.VMEM((bags, chunk), BF16),
            pltpu.VMEM((chunk, bags), BF16),
            pltpu.VMEM((2 * slots * 8, 128), F32),
            pltpu.VMEM((peers * 8, 128), I32),
            pltpu.VMEM((peers * 8, 128), I32),
            pltpu.VMEM((max(peers, 32) * slots, local_rows), BF16),
            pltpu.VMEM((peers * slots, width), BF16),
            pltpu.VMEM((peers * slots, width), BF16),
            pltpu.VMEM((peers * slots, width), BF16),
            pltpu.VMEM((peers * slots, width), BF16),
            pltpu.VMEM((samples, cross_width), BF16),
            pltpu.VMEM((bags, width), F32),
            pltpu.VMEM((samples, cross_width), F32),
            pltpu.VMEM((bags, width), BF16),
            pltpu.VMEM((groups, width, block), F32),
            pltpu.VMEM((pairs, width, block), F32),
            pltpu.VMEM((pairs, width, block), BF16),
            pltpu.VMEM((pairs, width, block), BF16),
            pltpu.VMEM((ring * 8, 128), F32),
            pltpu.VMEM((ring * 8, 128), F32),
            pltpu.VMEM((ring * 8, 128), F32),
            pltpu.VMEM((pairs * 8, 128), F32),
            pltpu.VMEM((16, 128), F32),
            dma((2,)),
            dma((peers,)),
            dma((peers,)),
            dma((peers,)),
            dma((peers,)),
            dma((peers,)),
            dma((peers,)),
            dma((pairs,)),
            dma((pairs,)),
            dma((pairs,)),
            dma((pairs,)),
            dma((pairs,)),
            dma((pairs,)),
            dma((pairs,)),
            dma((pairs,)),
            dma((5, max(ring, pairs))),
            dma((5, max(ring, pairs))),
        ],
        compiler_params=pltpu.CompilerParams(
            collective_id=0, has_side_effects=True, vmem_limit_bytes=60 * 1024 * 1024
        ),
    )(
        own, lengths, rows, labels.reshape(1, samples), sample_weight.reshape(1, samples), dense_part, table_window,
        cross_bias, head_w, down_w, up_w,
    )
    head_grad = sums[:tiles].reshape(cross_width)
    bias_grad = sums[tiles:2 * tiles].reshape(cross_width)
    return row_grad.astype(F32), head_grad, bias_grad, dense_grad


def solution(mesh):
    in_specs = (
        P("emb", None),
        P(("grp", "emb"), None),
        P(("grp", "emb"), None, None),
        P(("grp", "emb"), None),
        P(("grp", "emb"), None, None),
        P(("grp", "emb")),
        P(("grp", "emb")),
        P(),
        P(),
        P(),
        P(),
    )
    out_specs = (P("emb", None), P(), P(), P(("grp", "emb"), None))
    return jax.shard_map(body, mesh=mesh, in_specs=in_specs, out_specs=out_specs, check_vma=False)
```

```python
import functools

import jax
import jax.numpy as jnp
from jax import lax
from jax.experimental import pallas as pl
from jax.experimental.pallas import tpu as pltpu
from jax.sharding import PartitionSpec as P

MESH = pl.DeviceIdType.MESH
F32 = jnp.float32
BF16 = jnp.bfloat16
I32 = jnp.int32
I16 = jnp.int16
NT = (((1,), (1,)), ((), ()))
LAG = 3
UNROLL = 4


def iota(shape, dim):
    return lax.broadcasted_iota(I32, shape, dim)


def hot(mask):
    return jnp.where(mask, jnp.ones((), BF16), jnp.zeros((), BF16))


def wide(row):
    return jnp.broadcast_to(row, (16, row.shape[1])).astype(I16)


def hot_rows(index, row):
    rows, lanes = index.shape[0], row.shape[1]
    parts = []
    for a in range(0, lanes, 128):
        parts.append(hot(index.reshape(rows // 16, 16, 128) == wide(row[:, a:a + 128])[None]).reshape(rows, 128))
    return jnp.concatenate(parts, axis=1) if len(parts) > 1 else parts[0]


def kernel(
    ring, tables, slots, pairs,
    own_ref, len_ref, rows_ref, label_ref, weight_ref, dense_ref, table_ref, bias_ref, head_ref,
    down_any, up_any,
    rg_ref, hb_ref, dg_ref,
    down, up, pos_row, slot_row, pos_col, owners, pick, turned_pick, req_acc, code_s, code_r, counts, pool_s, pool_r, grad_s, grad_r,
    x0, x0_acc, cross, d_pool, acc, pair_r, rs_s, rs_r,
    hb, h1, h2, h3, h4,
    w_sem, code_ss, code_rs, pool_ss, pool_rs, grad_ss, grad_rs,
    pr_ss, pr_rs, rs_ss, rs_rs, ag_ss, ag_rs, pa_ss, pa_rs, h_ss, h_rs,
):
    peers = ring * ring
    groups = 2 * pairs
    chunk = ring * slots
    bits = ring.bit_length() - 1
    code_rows = slots * 8 // 128
    local_rows, width = table_ref.shape
    block = local_rows // groups
    tiles = tables + 1
    me = lax.axis_index("emb")
    grp = lax.axis_index("grp")
    x, z = me // ring, lax.rem(me, ring)
    y, c = grp // 2, lax.rem(grp, 2)
    mate = {"grp": grp + 1 - 2 * c}

    def ahead(k):
        dx = lax.rem(3 * k, ring)
        dz = lax.rem(3 * (k // ring) + ring - dx, ring)
        return {"emb": lax.rem(x + dx, ring) * ring + lax.rem(z + dz, ring)}

    def behind(k):
        dx = lax.rem(3 * k, ring)
        dz = lax.rem(3 * (k // ring) + ring - dx, ring)
        return {"emb": lax.rem(x + ring - dx, ring) * ring + lax.rem(z + ring - dz, ring)}

    def along_x(d):
        return {"emb": lax.rem(x + d, ring) * ring + z}

    def along_z(d):
        return {"emb": x * ring + lax.rem(z + d, ring)}

    def along_y(d):
        return {"grp": lax.rem(y + d, pairs) * 2 + c}

    def remote(src, dst, send, recv, where):
        return pltpu.make_async_remote_copy(
            src_ref=src, dst_ref=dst, send_sem=send, recv_sem=recv, device_id=where, device_id_type=MESH
        )

    def loop(low, high, step):
        def run(i, carry):
            step(i)
            return carry

        lax.fori_loop(low, high, run, 0)

    down_copy = pltpu.make_async_copy(down_any, down, w_sem.at[0])
    up_copy = pltpu.make_async_copy(up_any, up, w_sem.at[1])
    down_copy.start()
    up_copy.start()

    barrier = pltpu.get_barrier_semaphore()
    loop(1, peers, lambda k: pl.semaphore_signal(barrier, inc=1, device_id=ahead(k), device_id_type=MESH))
    loop(1, pairs, lambda d: pl.semaphore_signal(barrier, inc=1, device_id=along_y(d), device_id_type=MESH))
    pl.semaphore_signal(barrier, inc=1, device_id=mate, device_id_type=MESH)

    number = iota((max(chunk, 256), 128), 0).astype(I16)
    lane = iota((16, 128), 1).astype(I16)
    upper = jnp.concatenate(
        [
            jnp.where(iota((128, 128), 0) < iota((128, 128), 1), 1.0, 0.0).astype(BF16),
            jnp.ones((128, 128), BF16),
        ],
        axis=1,
    )
    half = tables // 2
    names = slots * 8

    def bucket(t, carry):
        owner = own_ref[pl.ds(t, 1), :]
        dx = ((owner >> bits) - x) & (ring - 1)
        dz = ((owner & (ring - 1)) - z) & (ring - 1)
        kind = ((3 * (dz + dx)) & (ring - 1)) * ring + ((3 * dx) & (ring - 1))
        mine = jnp.where(iota((128, 128), 0) == kind, 1.0, 0.0)
        mine_b = mine.astype(BF16)
        owners[t // half, :, pl.ds(pl.multiple_of(lax.rem(t, half) * 128, 128), 128)] = mine_b
        sums = jnp.dot(mine_b, upper, preferred_element_type=F32)
        slot = jnp.sum(mine * (sums[:, :128] + carry), axis=0, keepdims=True).astype(I32)
        pos_row[pl.ds(t, 1), :] = kind * slots + slot
        slot_row[pl.ds(t, 1), :] = slot
        return carry + sums[:, 128:]

    lax.fori_loop(0, tables, bucket, jnp.zeros((128, 128), F32), unroll=2)

    def spread(t):
        slot = slot_row[pl.ds(t, 1), :]
        live = iota((8, 128), 0) < len_ref[pl.ds(t, 1), :]
        code = jnp.where(live, rows_ref[pl.ds(pl.multiple_of(t * 8, 8), 8), :] + 1, 0)
        here = iota((slots, 8, 128), 0) == slot[None]
        top = pl.multiple_of((t // half) * 2 * names, 16)
        lanes = pl.ds(pl.multiple_of(lax.rem(t, half) * 128, 128), 128)
        for part, at in ((code >> 4, 0), (code & 15, names)):
            value = jnp.where(here, part.astype(F32)[None], 0.0).reshape(names, 128).astype(BF16)
            counts[pl.ds(top + at, names), lanes] = value

    loop(0, tables, spread)
    req = lax.dot_general(counts[0:2 * names, 0:half * 128], owners[0], NT, preferred_element_type=F32)
    req_acc[...] = req
    req = lax.dot_general(counts[2 * names:4 * names, 0:half * 128], owners[1], NT, preferred_element_type=F32)
    req_acc[...] += req
    for p in range(code_rows):
        high = req_acc[p * 128:(p + 1) * 128, :]
        low = req_acc[names + p * 128:names + (p + 1) * 128, :]
        tile = (high * 16.0 + low - 1.0).T
        code_s[pl.ds(p, peers, stride=8), :] = tile[:peers].astype(I32)

    pl.semaphore_wait(barrier, peers - 1 + pairs - 1 + 1)

    def code_copy(k):
        part = pl.ds(pl.multiple_of(k * 8, 8), code_rows)
        return remote(code_s.at[part], code_r.at[part], code_ss.at[k], code_rs.at[k], ahead(k))

    def pool_copy(k):
        part = pl.ds(pl.multiple_of(k * slots, 16), slots)
        return remote(pool_s.at[part], pool_r.at[part], pool_ss.at[k], pool_rs.at[k], behind(k))

    def grad_copy(k):
        part = pl.ds(pl.multiple_of(k * slots, 16), slots)
        return remote(grad_s.at[part], grad_r.at[part], grad_ss.at[k], grad_rs.at[k], ahead(k))

    loop(1, peers, lambda k: code_copy(k).start())
    code_r[0:8, :] = code_s[0:8, :]

    def turn(t):
        row = jnp.broadcast_to(pos_row[pl.ds(t, 1), :], (128, 128)).astype(F32)
        pos_col[pl.ds(pl.multiple_of(t * 128, 128), 128), :] = row.T.astype(I32).astype(I16)
        x0_acc[pl.ds(pl.multiple_of(t * 128, 128), 128), :] = jnp.zeros((128, 128), F32)


    def count_bags(k):
        tile = code_r[pl.ds(pl.multiple_of(k * 8, 8), 8), :]
        base = pl.multiple_of(k * slots, 16)
        for first in range(0, code_rows, 2):
            last = min(first + 2, code_rows)
            code = jnp.concatenate([tile[p:p + 1, :] for p in range(first, last)], axis=1)
            bags = (last - first) * 16
            lanes = bags * 8
            spans = local_rows // 256
            key = (code >> 8) * bags + (iota((1, lanes), 1) >> 3)
            left = hot_rows(number[:spans * bags], key)
            right = hot_rows(number[:256], code & 255)
            out = lax.dot_general(left, right, NT, preferred_element_type=F32).astype(BF16)
            for s in range(spans):
                counts[pl.ds(base + first * 16, bags), s * 256:(s + 1) * 256] = out[s * bags:(s + 1) * bags, :]

    def pool_chunk(j):
        def one(n):
            first = j * ring + n * UNROLL

            @pl.when(first != 0)
            def _():
                code_copy(first).wait_recv()

            for i in range(1, UNROLL):
                code_copy(first + i).wait_recv()
            for i in range(UNROLL):
                count_bags(first + i)

        loop(0, ring // UNROLL, one)
        part = pl.ds(pl.multiple_of(j * chunk, 16), chunk)
        pool_s[part, :] = jnp.dot(counts[part, :], table_ref[...], preferred_element_type=F32).astype(BF16)

        def send(i):
            k = j * ring + i

            @pl.when(k != 0)
            def _():
                pool_copy(k).start()

        loop(0, ring, send)

        @pl.when(j == 0)
        def _():
            pool_r[0:slots, :] = pool_s[0:slots, :]

    def place_pair(j):
        def one(i):
            k = j * 2 * ring + i

            @pl.when(k != 0)
            def _():
                pool_copy(k).wait_recv()

        loop(0, 2 * ring, one)
        base = pl.multiple_of(j * 2 * chunk, 16)
        offset = base.astype(I16)

        def some(t):
            rows = pl.ds(pl.multiple_of(t * 256, 256), 256)
            column = (pos_col[rows, :] - offset).reshape(16, 16, 128)
            column = jnp.where(column >= chunk, column - chunk, column)
            for q in range(0, chunk, 128):
                pick[rows, q:q + 128] = hot(column == (lane + q)[None]).reshape(256, 128)

        loop(0, tables // 2, some)
        right = jnp.concatenate([pool_r[pl.ds(base, chunk), :], pool_r[pl.ds(base + chunk, chunk), :]], axis=1)

        def apply(n):
            rows = pl.ds(pl.multiple_of(n * half * 128, 128), half * 128)
            out = jnp.dot(pick[rows, :], right, preferred_element_type=F32)
            first = pos_col[rows, :].astype(I32) < base + chunk
            x0_acc[rows, :] += jnp.where(first, out[:, :width], out[:, width:])

        loop(0, 2, apply)

    def forward(j):
        pool_chunk(j)

        @pl.when(j == 1)
        def _():
            loop(0, tables, turn)
            acc[...] = jnp.zeros_like(acc)

        if ring >= 8:

            @pl.when((j >= 5) & (lax.rem(j, 2) == 1))
            def _():
                place_pair((j - 5) // 2)

    loop(0, ring, forward)
    loop(ring // 2 - 2 if ring >= 8 else 0, ring // 2, place_pair)

    down_copy.wait()
    up_copy.wait()
    x0[:, :width] = dense_ref[...]
    for t in range(tables):
        x0[:, (t + 1) * width:(t + 2) * width] = x0_acc[t * 128:(t + 1) * 128, :].astype(BF16)
    step = 3 * width
    cuts = range(0, tiles * width, step)
    low = jnp.dot(x0[...], down[...], preferred_element_type=F32).astype(BF16)
    logit_acc = jnp.zeros((128, width), F32)
    for a in cuts:
        part = jnp.dot(low, up[:, a:a + step], preferred_element_type=F32) + bias_ref[a:a + step].reshape(1, step)
        cross[:, a:a + step] = part
        x0f = x0[:, a:a + step].astype(F32)
        term = (x0f * part + x0f) * head_ref[a:a + step].reshape(1, step)
        for b in range(0, step, width):
            logit_acc = logit_acc + term[:, b:b + width]
    logit = jnp.sum(logit_acc, axis=1, keepdims=True)
    label = jnp.broadcast_to(label_ref[...].astype(F32), (128, 128)).T[:, 0:1]
    weight = jnp.broadcast_to(weight_ref[...], (128, 128)).T[:, 0:1]
    dlogit = weight * (jax.nn.sigmoid(logit) - label)
    hb[...] = jnp.zeros_like(hb)
    for a in cuts:
        x0f = x0[:, a:a + step].astype(F32)
        x1 = x0f * cross[:, a:a + step] + x0f
        d_cross = dlogit * head_ref[a:a + step].reshape(1, step) * x0f
        head_part = jnp.sum(dlogit * x1, axis=0, keepdims=True)
        bias_part = jnp.sum(d_cross, axis=0, keepdims=True)
        for b in range(0, step, width):
            r = (a + b) // width
            hb[r:r + 1, :] = head_part[:, b:b + width]
            hb[tiles + r:tiles + r + 1, :] = bias_part[:, b:b + width]
        x0[:, a:a + step] = d_cross.astype(BF16)
    d_low = lax.dot_general(x0[...], up[...], NT, preferred_element_type=F32).astype(BF16)

    def h_part(r):
        return pl.ds(pl.multiple_of(r * 8, 8), 8)

    def h1_copy(d):
        return remote(hb.at[h_part(lax.rem(x + d, ring))], h1.at[h_part(d)], h_ss.at[0, d], h_rs.at[0, d], along_x(d))

    def h2_copy(d):
        return remote(h2.at[h_part(z)], h2.at[h_part(z)], h_ss.at[1, d], h_rs.at[1, d], along_z(d))

    def h3_copy(d):
        return remote(h3.at[h_part(y)], h3.at[h_part(y)], h_ss.at[2, d], h_rs.at[2, d], along_y(d))

    def h4_copy():
        return remote(h4.at[h_part(c)], h4.at[h_part(c)], h_ss.at[3, 0], h_rs.at[3, 0], mate)

    def h5_copy(d):
        return remote(hb_ref.at[h_part(x)], hb_ref.at[h_part(x)], h_ss.at[4, d], h_rs.at[4, d], along_x(d))

    loop(1, ring, lambda d: h1_copy(d).start())

    def total_of(ref, count, start=0):
        total = ref[start * 8:start * 8 + 8, :]
        for r in range(start + 1, count):
            total = total + ref[r * 8:r * 8 + 8, :]
        return total

    def h_step1():
        loop(1, ring, lambda d: h1_copy(d).wait_recv())
        h2[h_part(z), :] = total_of(h1, ring, 1) + hb[h_part(x), :]
        loop(1, ring, lambda d: h2_copy(d).start())

    def h_step2():
        loop(1, ring, lambda d: h2_copy(d).wait_recv())
        h3[h_part(y), :] = total_of(h2, ring)
        loop(1, pairs, lambda d: h3_copy(d).start())

    def h_step3():
        loop(1, pairs, lambda d: h3_copy(d).wait_recv())
        h4[h_part(c), :] = total_of(h3, pairs)
        h4_copy().start()

    def h_step4():
        h4_copy().wait_recv()
        hb_ref[h_part(x), :] = total_of(h4, 2)
        loop(1, ring, lambda d: h5_copy(d).start())

    for a in cuts:
        d_x1 = dlogit * head_ref[a:a + step].reshape(1, step)
        d_x0 = d_x1 * (cross[:, a:a + step] + 1.0) + lax.dot_general(
            d_low, down[a:a + step, :], NT, preferred_element_type=F32
        )
        d_x0 = d_x0.astype(BF16)
        for b in range(0, step, width):
            t = (a + b) // width - 1
            if t < 0:
                dg_ref[...] = d_x0[:, b:b + width]
            else:
                d_pool[t * 128:(t + 1) * 128, :] = d_x0[:, b:b + width]

    def grad_chunk(j):
        def some(t):
            for h in range(2):
                lanes = pl.ds(pl.multiple_of(t * 256 + h * 128, 128), 128)
                turned_pick[:, lanes] = hot_rows(number[:chunk], pos_row[pl.ds(t * 2 + h, 1), :] - j * chunk)

        loop(0, tables // 2, some)
        out = jnp.dot(turned_pick[...], d_pool[...], preferred_element_type=F32)
        grad_s[pl.ds(pl.multiple_of(j * chunk, 16), chunk), :] = out.astype(BF16)

        def send(i):
            k = j * ring + i

            @pl.when(k != 0)
            def _():
                grad_copy(k).start()

        loop(0, ring, send)

        @pl.when(j == 0)
        def _():
            grad_r[0:slots, :] = grad_s[0:slots, :]

    def row_chunk(j):
        def one(i):
            k = j * ring + i

            @pl.when(k != 0)
            def _():
                grad_copy(k).wait_recv()

        loop(0, ring, one)
        part = pl.ds(pl.multiple_of(j * chunk, 16), chunk)
        turned = grad_r[part, :].astype(F32).T.astype(BF16)
        for b in range(0, local_rows, 256):
            out = jnp.dot(turned, counts[part, b:b + 256], preferred_element_type=F32)
            for a in range(0, 256, 128):
                g, at = (a + b) // block, (a + b) % block
                acc[g, :, at:at + 128] += out[:, a:a + 128]

    def backward(j):
        grad_chunk(j)

        @pl.when(j >= LAG)
        def _():
            row_chunk(j - LAG)

    loop(0, ring, backward)
    h_step1()
    h_step2()
    loop(ring - LAG, ring, row_chunk)

    def pr_copy(d):
        r = lax.rem(y + d, pairs)
        return remote(acc.at[(1 - c) * pairs + r], pair_r.at[r], pr_ss.at[d], pr_rs.at[d], mate)

    def rs_copy(d):
        return remote(rs_s.at[lax.rem(y + d, pairs)], rs_r.at[d], rs_ss.at[d], rs_rs.at[d], along_y(d))

    def out_block(side, r):
        return rg_ref.at[pl.ds(pl.multiple_of((side * pairs + r) * block, block), block)]

    def ag_copy(d):
        here = out_block(c, y)
        return remote(here, here, ag_ss.at[d], ag_rs.at[d], along_y(d))

    def pa_copy(d):
        here = out_block(c, lax.rem(y + pairs - d, pairs))
        return remote(here, here, pa_ss.at[d], pa_rs.at[d], mate)

    loop(0, pairs, lambda d: pr_copy(lax.rem(d + 1, pairs)).start())

    def pair_sum(n):
        d = lax.rem(n + 1, pairs)
        pr_copy(d).wait_recv()
        r = lax.rem(y + d, pairs)
        both = pair_r[r] + acc[c * pairs + r]
        pair_r[r] = both
        rs_s[r] = both.astype(BF16)

        @pl.when(d != 0)
        def _():
            rs_copy(d).start()

    loop(0, pairs, pair_sum)
    h_step3()
    loop(1, pairs, lambda d: rs_copy(d).wait_recv())
    total = pair_r[y]
    for d in range(1, pairs):
        total = total + rs_r[d].astype(F32)
    rg_ref[pl.ds(pl.multiple_of((c * pairs + y) * block, block), block), :] = total.T.astype(BF16)
    loop(1, pairs, lambda d: ag_copy(d).start())
    pa_copy(0).start()
    h_step4()

    def forward_block(d):
        ag_copy(d).wait_recv()
        pa_copy(d).start()

    loop(1, pairs, forward_block)
    loop(0, pairs, lambda d: pa_copy(d).wait_recv())
    loop(1, ring, lambda d: h5_copy(d).wait_recv())

    def sent(k):
        code_copy(k).wait_send()
        pool_copy(k).wait_send()
        grad_copy(k).wait_send()

    loop(1, peers, sent)

    def sent_x(d):
        h1_copy(d).wait_send()
        h2_copy(d).wait_send()
        h5_copy(d).wait_send()

    loop(1, ring, sent_x)

    def sent_y(d):
        h3_copy(d).wait_send()
        rs_copy(d).wait_send()
        ag_copy(d).wait_send()

    loop(1, pairs, sent_y)

    def sent_pair(d):
        pr_copy(d).wait_send()
        pa_copy(d).wait_send()

    loop(0, pairs, sent_pair)
    h4_copy().wait_send()


def body(
    table_window, dense_part, bag_rows, bag_lengths, bag_owner, labels, sample_weight, down_w, up_w, cross_bias, head_w
):
    peers = lax.axis_size("emb")
    groups = lax.axis_size("grp")
    ring = 1
    while ring * ring < peers:
        ring *= 2
    pairs = groups // 2
    samples, width = dense_part.shape
    tables, entries = bag_rows.shape[1:]
    local_rows = table_window.shape[0]
    cross_width, rank = down_w.shape
    capacity = samples * tables * 3 // (2 * peers)
    slots = -(-capacity // 16) * 16
    chunk = ring * slots
    bags = samples * tables
    block = local_rows // groups
    tiles = cross_width // width
    own = bag_owner.reshape(samples, tables).T
    lengths = bag_lengths.T
    rows = bag_rows.transpose(1, 2, 0).reshape(tables * entries, samples)
    vmem = pl.BlockSpec(memory_space=pltpu.VMEM)
    hbm = pl.BlockSpec(memory_space=pl.ANY)
    dma = pltpu.SemaphoreType.DMA
    row_grad, sums, dense_grad = pl.pallas_call(
        functools.partial(kernel, ring, tables, slots, pairs),
        out_shape=(
            jax.ShapeDtypeStruct((local_rows, width), BF16),
            jax.ShapeDtypeStruct((ring * 8, width), F32),
            jax.ShapeDtypeStruct((samples, width), BF16),
        ),
        in_specs=[vmem] * 9 + [hbm] * 2,
        out_specs=(vmem, vmem, vmem),
        scratch_shapes=[
            pltpu.VMEM((cross_width, rank), BF16),
            pltpu.VMEM((rank, cross_width), BF16),
            pltpu.VMEM((-(-tables // 8) * 8, 128), I32),
            pltpu.VMEM((-(-tables // 8) * 8, 128), I32),
            pltpu.VMEM((bags, 128), I16),
            pltpu.VMEM((2, 128, bags // 2), BF16),
            pltpu.VMEM((bags, chunk), BF16),
            pltpu.VMEM((chunk, bags), BF16),
            pltpu.VMEM((2 * slots * 8, 128), F32),
            pltpu.VMEM((peers * 8, 128), I32),
            pltpu.VMEM((peers * 8, 128), I32),
            pltpu.VMEM((max(peers, 32) * slots, local_rows), BF16),
            pltpu.VMEM((peers * slots, width), BF16),
            pltpu.VMEM((peers * slots, width), BF16),
            pltpu.VMEM((peers * slots, width), BF16),
            pltpu.VMEM((peers * slots, width), BF16),
            pltpu.VMEM((samples, cross_width), BF16),
            pltpu.VMEM((bags, width), F32),
            pltpu.VMEM((samples, cross_width), F32),
            pltpu.VMEM((bags, width), BF16),
            pltpu.VMEM((groups, width, block), F32),
            pltpu.VMEM((pairs, width, block), F32),
            pltpu.VMEM((pairs, width, block), BF16),
            pltpu.VMEM((pairs, width, block), BF16),
            pltpu.VMEM((ring * 8, 128), F32),
            pltpu.VMEM((ring * 8, 128), F32),
            pltpu.VMEM((ring * 8, 128), F32),
            pltpu.VMEM((pairs * 8, 128), F32),
            pltpu.VMEM((16, 128), F32),
            dma((2,)),
            dma((peers,)),
            dma((peers,)),
            dma((peers,)),
            dma((peers,)),
            dma((peers,)),
            dma((peers,)),
            dma((pairs,)),
            dma((pairs,)),
            dma((pairs,)),
            dma((pairs,)),
            dma((pairs,)),
            dma((pairs,)),
            dma((pairs,)),
            dma((pairs,)),
            dma((5, max(ring, pairs))),
            dma((5, max(ring, pairs))),
        ],
        compiler_params=pltpu.CompilerParams(
            collective_id=0, has_side_effects=True, vmem_limit_bytes=60 * 1024 * 1024
        ),
    )(
        own, lengths, rows, labels.reshape(1, samples), sample_weight.reshape(1, samples), dense_part, table_window,
        cross_bias, head_w, down_w, up_w,
    )
    head_grad = sums[:tiles].reshape(cross_width)
    bias_grad = sums[tiles:2 * tiles].reshape(cross_width)
    return row_grad.astype(F32), head_grad, bias_grad, dense_grad


def solution(mesh):
    in_specs = (
        P("emb", None),
        P(("grp", "emb"), None),
        P(("grp", "emb"), None, None),
        P(("grp", "emb"), None),
        P(("grp", "emb"), None, None),
        P(("grp", "emb")),
        P(("grp", "emb")),
        P(),
        P(),
        P(),
        P(),
    )
    out_specs = (P("emb", None), P(), P(), P(("grp", "emb"), None))
    return jax.shard_map(body, mesh=mesh, in_specs=in_specs, out_specs=out_specs, check_vma=False)
```
